32 devices in a mesh: row: 4 (over y, x), col: 8 (over z, core).
Axes of the slice: x: 2, y: 2, z: 4, core: 2. Of those that a mesh axis runs over, the one named last changes fastest.
Arguments:
- upper_tiles: bfloat16 [256, 5, 256, 256], P('row', None, 'col'), may hold values from -0.8984375 to 0.8984375
- occupied: int32 [256, 4], P(('row', 'col')), may hold values from 0 to 1, as said below
Outputs:
- square_tiles: bfloat16 [256, 5, 256, 256], P('row', None, 'col')
The draws below stay inside these ranges and needn't reach their ends.
Inputs may be any that keep to these rules, and one draw needn't show every extreme that they name: Occupancy; its density differs between aligned groups of 8 block rows, and the diagonal block is always occupied (not listed).
All inputs are finite; a program needn't handle non-finite values.
Results may differ from the reference program's by a relative error of at most 0.0024.
Values may be sent and summed in bfloat16 or wider, within the bound.
A program may use at most 256 MiB of HBM per device.

```python
import jax
import jax.numpy as jnp
from jax import lax

BLOCK = 256
BAND = 4
R_DEV = 8
NB = 256


def draw_occupied(key, part):
    level_key = jax.random.fold_in(key, 11)
    cell_key = jax.random.fold_in(key, 23)
    levels = jax.random.randint(level_key, (NB // R_DEV, 1), 1, 10)
    levels = jnp.repeat(levels, R_DEV, axis=0)
    cells = jax.random.randint(cell_key, (NB, BAND), 0, 10)
    return (cells < levels).astype(jnp.int32)


def steps_of(stream_key, extent, split, smallest, high):
    factor_of, own = 1.0, jax.random.fold_in(stream_key, 6)
    for dim, blocks in split:
        steps = jnp.exp(jax.random.uniform(jax.random.fold_in(own, dim), (blocks,), jnp.float32, smallest / len(split), high / len(split)))
        factor_of = factor_of * jnp.repeat(steps, extent[dim] // blocks).reshape([-1 if axis == dim else 1 for axis in range(len(extent))])
    return factor_of


def noise(stream_key, shape, spread, bound, shards=(), kind=jnp.bfloat16):
    values = spread * jax.random.normal(stream_key, shape, jnp.float32)
    if shards:
        values = values * steps_of(stream_key, shape, shards, -0.22, 0.18)
    return jnp.clip(values, -bound, bound).astype(kind)


def setup_inputs(seed: int = 0) -> dict:
    key_of = jax.random.split(jax.random.key(seed), 3)
    upper_tiles = noise(key_of[0], (NB, BAND + 1, BLOCK, BLOCK), 0.15, 0.8984375, ((0, 4), (2, 8)))
    occupied = draw_occupied(jax.random.fold_in(key_of[2], 71), 0)
    return dict(upper_tiles=upper_tiles, occupied=occupied)


def build_band(upper_tiles, occupied, first_row, total_rows):
    block_rows = occupied.shape[0]
    band_width = occupied.shape[1]
    row_index = first_row + jnp.arange(block_rows, dtype=jnp.int32)
    offsets = jnp.arange(1, band_width + 1, dtype=jnp.int32)
    kept_mask = (occupied == 1) & (row_index[:, None] + offsets[None, :] < total_rows)
    diag_full = upper_tiles[:, 0].astype(jnp.float32)
    diag_tile = (0.5 * (diag_full + jnp.swapaxes(diag_full, 1, 2))).astype(jnp.bfloat16)
    off_tiles = jnp.where(kept_mask[:, :, None, None], upper_tiles[:, 1:], jnp.zeros((), jnp.bfloat16))
    return jnp.concatenate([diag_tile[:, None], off_tiles], axis=1), kept_mask


def square_band(extended, kept_mask, block_rows, band_width):
    results = []
    for column_shift in range(band_width + 1):
        lefts = []
        rights = []
        for inner in range(column_shift - band_width, band_width + 1):
            start = band_width + inner
            if inner >= 0:
                left = extended[band_width:band_width + block_rows, inner]
            else:
                left = jnp.swapaxes(extended[start:start + block_rows, -inner], 1, 2)
            rest = column_shift - inner
            if rest >= 0:
                right = extended[start:start + block_rows, rest]
            else:
                lower = band_width + column_shift
                right = jnp.swapaxes(extended[lower:lower + block_rows, -rest], 1, 2)
            lefts.append(left)
            rights.append(right)
        left_stack = jnp.stack(lefts, axis=1).astype(jnp.float32)
        right_stack = jnp.stack(rights, axis=1).astype(jnp.float32)
        summed = jnp.einsum("rkab,rkbc->rac", left_stack, right_stack)
        if column_shift > 0:
            summed = jnp.where(kept_mask[:, column_shift - 1, None, None], summed, jnp.zeros((), jnp.float32))
        results.append(summed.astype(jnp.bfloat16))
    return jnp.stack(results, axis=1)


def reference(upper_tiles, occupied):
    groups = NB // R_DEV
    window = R_DEV + 2 * BAND

    def one_group(group):
        first = group * R_DEV - BAND
        rows = first + jnp.arange(window, dtype=jnp.int32)
        valid = (rows >= 0) & (rows < NB)
        index = jnp.clip(rows, 0, NB - 1).astype(jnp.int32)
        tiles = upper_tiles[index]
        occ = occupied[index]
        band, kept_mask = build_band(tiles, occ, first, NB)
        band = jnp.where(valid[:, None, None, None], band, jnp.zeros((), band.dtype))
        return square_band(band, kept_mask[BAND:BAND + R_DEV], R_DEV, BAND)

    stacked = lax.map(one_group, jnp.arange(groups, dtype=jnp.int32))
    return stacked.reshape((NB,) + stacked.shape[2:])
```

```python
import functools

import jax
import jax.numpy as jnp
from jax import lax
from jax.experimental import pallas as pl
from jax.experimental.pallas import tpu as pltpu
from jax.sharding import PartitionSpec as P

MESH = pl.DeviceIdType.MESH


def band_square_kernel(
    rows_n,
    cols_n,
    width,
    up,
    occ,
    out,
    tiles,
    strip,
    prod,
    occ_v,
    kept,
    in_send,
    in_recv,
    halo_send,
    halo_recv,
    out_send,
    out_recv,
    occ_sem,
    loc_sem,
):
    block_rows, block = tiles.shape[0], tiles.shape[2]
    slab = block // cols_n
    row, col = lax.axis_index("row"), lax.axis_index("col")
    odd = lax.rem(row, 2)

    def turned(c):
        return jnp.where(odd == 1, cols_n - 1 - c, c)

    pos = turned(col)
    chunk = row * cols_n + pos
    step = 1 - 2 * odd
    has_next, has_prev = chunk < rows_n * cols_n - 1, chunk > 0
    next_out, prev_out = pos == cols_n - 1, pos == 0
    next_dev = (jnp.where(next_out, row + 1, row), jnp.where(next_out, col, col + step))
    prev_dev = (jnp.where(prev_out, row - 1, row), jnp.where(prev_out, col, col - step))

    def other(k):
        return lax.rem(col + k, cols_n)

    barrier = pltpu.get_barrier_semaphore()

    @pl.loop(1, cols_n)
    def _(k):
        pl.semaphore_signal(barrier, inc=1, device_id=(row, other(k)), device_id_type=MESH)

    @pl.when(next_out & has_next)
    def _():
        pl.semaphore_signal(barrier, inc=1, device_id=next_dev, device_id_type=MESH)

    @pl.when(prev_out & has_prev)
    def _():
        pl.semaphore_signal(barrier, inc=1, device_id=prev_dev, device_id_type=MESH)

    outside = (next_out & has_next) | (prev_out & has_prev)
    pl.semaphore_wait(barrier, cols_n - 1 + jnp.where(outside, 1, 0))

    def slab_of(c):
        return pl.ds(pl.multiple_of(c * slab, slab), slab)

    def spans(part):
        for r in range(block_rows):
            cut = width - r if r < width else block_rows - r
            first = r < width
            yield r, (0 if first == (part == 0) else cut), (cut if first == (part == 0) else width + 1)

    mine = slab_of(col)
    for part in range(2):
        for r, lo, hi in spans(part):
            pltpu.make_async_copy(
                up.at[pos * block_rows + r, lo:hi], tiles.at[r, lo:hi, mine, :], loc_sem.at[part]
            ).start()

            @pl.loop(1, cols_n)
            def _(k):
                dst = other(k)
                pltpu.make_async_remote_copy(
                    src_ref=up.at[turned(dst) * block_rows + r, lo:hi],
                    dst_ref=tiles.at[r, lo:hi, mine, :],
                    send_sem=in_send.at[dst],
                    recv_sem=in_recv.at[part, col],
                    device_id=(row, dst),
                    device_id_type=MESH,
                ).start()

    partner = cols_n - 1 - col
    occ_copy = pltpu.make_async_remote_copy(
        src_ref=occ,
        dst_ref=occ_v,
        send_sem=occ_sem.at[0],
        recv_sem=occ_sem.at[1],
        device_id=(row, partner),
        device_id_type=MESH,
    )

    @pl.when(odd == 1)
    def _():
        occ_copy.start()
        occ_copy.wait()

    @pl.when(odd == 0)
    def _():
        here = pltpu.make_async_copy(occ, occ_v, occ_sem.at[1])
        here.start()
        here.wait()

    shape = occ_v.shape
    index = (
        chunk * block_rows
        + lax.broadcasted_iota(jnp.int32, shape, 0)
        + lax.broadcasted_iota(jnp.int32, shape, 1)
        + 1
    )
    total = rows_n * cols_n * block_rows
    kept[...] = jnp.where((occ_v[...] == 1) & (index < total), 1, 0)

    def part_of(n):
        return slice(n * block, (n + 1) * block)

    @pl.when(jnp.logical_not(has_prev))
    def _():
        for q in range(width):
            strip[q, :, : (width - q) * block] = jnp.zeros(
                (block, (width - q) * block), strip.dtype
            )

    @pl.when(jnp.logical_not(has_next))
    def _():
        for m in range(width):
            strip[block_rows + m, :, width * block : (2 * width - m) * block] = jnp.zeros(
                (block, (width - m) * block), strip.dtype
            )

    def place(part):
        half = pl.ds(0, width)
        piece = tiles.at[half, :, mine, :]
        pltpu.make_async_copy(piece, piece, loc_sem.at[part]).wait()

        @pl.loop(1, cols_n)
        def _(k):
            src = other(k)
            piece = tiles.at[half, :, slab_of(src), :]
            pltpu.make_async_copy(piece, piece, in_recv.at[part, src]).wait()

        for d in range(width + 1):

            @pl.loop(part * width, (part + 1) * width)
            def _(j):
                r = lax.rem(j + block_rows - d, block_rows)
                tile = tiles[r, d]
                if d == 0:
                    full = tile.astype(jnp.float32)
                    strip[r, :, part_of(width)] = (0.5 * (full + full.T)).astype(strip.dtype)
                else:
                    flag = kept[pl.ds(r, 1), :][:, d - 1 : d]
                    tile = jnp.where(flag == 1, tile, jnp.zeros_like(tile))
                    strip[r, :, part_of(width + d)] = tile
                    strip[r + d, :, part_of(width - d)] = tile.T

    def halo(way, m):
        if way == 0:
            cut = slice(0, (width - m) * block)
            src, dst, dev = block_rows + m, m, next_dev
        else:
            cut = slice(width * block, (2 * width - m) * block)
            src, dst, dev = m, block_rows + m, prev_dev
        return pltpu.make_async_remote_copy(
            src_ref=strip.at[src, :, cut],
            dst_ref=strip.at[dst, :, cut],
            send_sem=halo_send.at[way, m],
            recv_sem=halo_recv.at[way, m],
            device_id=dev,
            device_id_type=MESH,
        )

    place(0)

    @pl.when(has_next)
    def _():
        for m in range(width):
            halo(0, m).start()

    @pl.when(has_prev)
    def _():
        for m in range(width):
            halo(1, m).start()

    place(1)

    @pl.when(has_prev)
    def _():
        for m in range(width):
            halo(0, m).wait_recv()

    @pl.when(has_next)
    def _():
        for m in range(width):
            halo(1, m).wait_recv()

    for d in range(1, width):

        @pl.loop(block_rows, block_rows + width - d)
        def _(r):
            strip[r + d, :, part_of(width - d)] = strip[r, :, part_of(width + d)].T

    @pl.loop(0, block_rows)
    def _(r):
        flags = kept[pl.ds(r, 1), :]
        for e in range(width + 1):
            value = lax.dot_general(
                strip[r, :, e * block :],
                strip[r + e, :, : (2 * width + 1 - e) * block],
                (((1,), (1,)), ((), ())),
                preferred_element_type=jnp.float32,
            )
            if e > 0:
                value = jnp.where(flags[:, e - 1 : e] == 1, value, 0.0)
            prod[r, e] = value.astype(prod.dtype)
        place_row = pos * block_rows + r
        pltpu.make_async_copy(prod.at[r, :, mine, :], out.at[place_row], loc_sem.at[2]).start()

        @pl.loop(1, cols_n)
        def _(k):
            dst = other(k)
            pltpu.make_async_remote_copy(
                src_ref=prod.at[r, :, slab_of(dst), :],
                dst_ref=out.at[place_row],
                send_sem=out_send.at[dst],
                recv_sem=out_recv.at[col],
                device_id=(row, dst),
                device_id_type=MESH,
            ).start()

    @pl.when(has_next)
    def _():
        for m in range(width):
            halo(0, m).wait_send()

    @pl.when(has_prev)
    def _():
        for m in range(width):
            halo(1, m).wait_send()

    def rows_of(c):
        return pl.ds(turned(c) * block_rows, block_rows)

    whole = out.at[rows_of(col)]
    pltpu.make_async_copy(whole, whole, loc_sem.at[2]).wait()

    @pl.loop(1, cols_n)
    def _(k):
        dev = other(k)
        sent = up.at[rows_of(dev)]
        pltpu.make_async_copy(sent, sent, in_send.at[dev]).wait()
        left = prod.at[:, :, slab_of(dev), :]
        pltpu.make_async_copy(left, left, out_send.at[dev]).wait()
        came = out.at[rows_of(dev)]
        pltpu.make_async_copy(came, came, out_recv.at[dev]).wait()


def shards(rows_n, cols_n, upper_tiles, occupied):
    block_rows, width = occupied.shape
    block = upper_tiles.shape[3]
    flags = jnp.pad(occupied, ((0, 0), (0, 128 - width)))
    dma = pltpu.SemaphoreType.DMA
    return pl.pallas_call(
        functools.partial(band_square_kernel, rows_n, cols_n, width),
        out_shape=jax.ShapeDtypeStruct(upper_tiles.shape, upper_tiles.dtype),
        in_specs=[pl.BlockSpec(memory_space=pl.ANY)] * 2,
        out_specs=pl.BlockSpec(memory_space=pl.ANY),
        scratch_shapes=[
            pltpu.VMEM((block_rows, width + 1, block, block), jnp.bfloat16),
            pltpu.VMEM((block_rows + width, block, (2 * width + 1) * block), jnp.bfloat16),
            pltpu.VMEM((block_rows, width + 1, block, block), jnp.bfloat16),
            pltpu.VMEM((block_rows, 128), jnp.int32),
            pltpu.VMEM((block_rows, 128), jnp.int32),
            dma((cols_n,)),
            dma((2, cols_n)),
            dma((2, width)),
            dma((2, width)),
            dma((cols_n,)),
            dma((cols_n,)),
            dma((2,)),
            dma((3,)),
        ],
        compiler_params=pltpu.CompilerParams(
            collective_id=0, has_side_effects=True, vmem_limit_bytes=48 * 2**20
        ),
        cost_estimate=pl.CostEstimate(
            flops=2 * 35 * block_rows * block**3, bytes_accessed=2 * upper_tiles.size * 2, transcendentals=0
        ),
    )(upper_tiles, flags)


def solution(mesh):
    return jax.shard_map(
        functools.partial(shards, mesh.shape["row"], mesh.shape["col"]),
        mesh=mesh,
        in_specs=(P("row", None, "col", None), P(("row", "col"), None)),
        out_specs=P("row", None, "col", None),
        check_vma=False,
    )
```

```python
import functools

import jax
import jax.numpy as jnp
from jax import lax
from jax.experimental import pallas as pl
from jax.experimental.pallas import tpu as pltpu
from jax.sharding import PartitionSpec as P

MESH = pl.DeviceIdType.MESH


def band_square_kernel(
    rows_n,
    cols_n,
    width,
    up,
    occ,
    out,
    tiles,
    strip,
    prod,
    occ_v,
    kept,
    in_send,
    in_recv,
    halo_send,
    halo_recv,
    out_send,
    out_recv,
    occ_sem,
    loc_sem,
):
    block_rows, block = tiles.shape[0], tiles.shape[2]
    slab = block // cols_n
    row, col = lax.axis_index("row"), lax.axis_index("col")
    odd = lax.rem(row, 2)

    def turned(c):
        return jnp.where(odd == 1, cols_n - 1 - c, c)

    pos = turned(col)
    chunk = row * cols_n + pos
    step = 1 - 2 * odd
    has_next, has_prev = chunk < rows_n * cols_n - 1, chunk > 0
    next_out, prev_out = pos == cols_n - 1, pos == 0
    next_dev = (jnp.where(next_out, row + 1, row), jnp.where(next_out, col, col + step))
    prev_dev = (jnp.where(prev_out, row - 1, row), jnp.where(prev_out, col, col - step))

    def other(k):
        return lax.rem(col + k, cols_n)

    barrier = pltpu.get_barrier_semaphore()

    @pl.loop(1, cols_n)
    def _(k):
        pl.semaphore_signal(barrier, inc=1, device_id=(row, other(k)), device_id_type=MESH)

    @pl.when(next_out & has_next)
    def _():
        pl.semaphore_signal(barrier, inc=1, device_id=next_dev, device_id_type=MESH)

    @pl.when(prev_out & has_prev)
    def _():
        pl.semaphore_signal(barrier, inc=1, device_id=prev_dev, device_id_type=MESH)

    outside = (next_out & has_next) | (prev_out & has_prev)
    pl.semaphore_wait(barrier, cols_n - 1 + jnp.where(outside, 1, 0))

    def slab_of(c):
        return pl.ds(pl.multiple_of(c * slab, slab), slab)

    def cells(stage):
        for r in range(block_rows):
            cut = width - r if r < width else block_rows - r
            first, rest = (0, cut), (cut, width + 1)
            if r >= width:
                first, rest = rest, first
            if stage == 0:
                yield r, first
            elif (stage == 1) == (r <= width):
                yield r, rest

    def piece_of(stage, c):
        count = sum(hi - lo for _, (lo, hi) in cells(stage))
        deep = max(n for n in range(1, width + 2) if count % n == 0 and count // n <= block_rows)
        return tiles.at[: count // deep, :deep, slab_of(c), :]

    mine = slab_of(col)
    for stage in range(3):
        for r, (lo, hi) in cells(stage):
            pltpu.make_async_copy(
                up.at[pos * block_rows + r, lo:hi], tiles.at[r, lo:hi, mine, :], loc_sem.at[stage]
            ).start()

            @pl.loop(1, cols_n)
            def _(k):
                dst = other(k)
                pltpu.make_async_remote_copy(
                    src_ref=up.at[turned(dst) * block_rows + r, lo:hi],
                    dst_ref=tiles.at[r, lo:hi, mine, :],
                    send_sem=in_send.at[dst],
                    recv_sem=in_recv.at[stage, col],
                    device_id=(row, dst),
                    device_id_type=MESH,
                ).start()

    partner = cols_n - 1 - col
    occ_copy = pltpu.make_async_remote_copy(
        src_ref=occ,
        dst_ref=occ_v,
        send_sem=occ_sem.at[0],
        recv_sem=occ_sem.at[1],
        device_id=(row, partner),
        device_id_type=MESH,
    )

    @pl.when(odd == 1)
    def _():
        occ_copy.start()
        occ_copy.wait()

    @pl.when(odd == 0)
    def _():
        here = pltpu.make_async_copy(occ, occ_v, occ_sem.at[1])
        here.start()
        here.wait()

    shape = occ_v.shape
    index = (
        chunk * block_rows
        + lax.broadcasted_iota(jnp.int32, shape, 0)
        + lax.broadcasted_iota(jnp.int32, shape, 1)
        + 1
    )
    total = rows_n * cols_n * block_rows
    kept[...] = jnp.where((occ_v[...] == 1) & (index < total), 1, 0)

    def part_of(n):
        return slice(n * block, (n + 1) * block)

    @pl.when(jnp.logical_not(has_prev))
    def _():
        for q in range(width):
            strip[q, :, : (width - q) * block] = jnp.zeros(
                (block, (width - q) * block), strip.dtype
            )

    @pl.when(jnp.logical_not(has_next))
    def _():
        for m in range(width):
            strip[block_rows + m, :, width * block : (2 * width - m) * block] = jnp.zeros(
                (block, (width - m) * block), strip.dtype
            )

    def place(stage):
        piece = piece_of(stage, col)
        pltpu.make_async_copy(piece, piece, loc_sem.at[stage]).wait()

        @pl.loop(1, cols_n)
        def _(k):
            src = other(k)
            piece = piece_of(stage, src)
            pltpu.make_async_copy(piece, piece, in_recv.at[stage, src]).wait()

        for d in range(width + 1):
            if stage == 0:
                lo, hi = block_rows - d, block_rows - d + width
            elif stage == 1:
                lo, hi = width - d, min(width + 1, block_rows - d)
            else:
                lo, hi = width + 1, block_rows - d
            if lo >= hi:
                continue

            @pl.loop(lo, hi)
            def _(j):
                r = lax.rem(j, block_rows)
                tile = tiles[r, d]
                if d == 0:
                    full = tile.astype(jnp.float32)
                    strip[r, :, part_of(width)] = (0.5 * (full + full.T)).astype(strip.dtype)
                else:
                    flag = kept[pl.ds(r, 1), :][:, d - 1 : d]
                    tile = jnp.where(flag == 1, tile, jnp.zeros_like(tile))
                    strip[r, :, part_of(width + d)] = tile
                    strip[r + d, :, part_of(width - d)] = tile.T

    def halo(way, m):
        if way == 0:
            cut = slice(0, (width - m) * block)
            src, dst, dev = block_rows + m, m, next_dev
        else:
            cut = slice(width * block, (2 * width - m) * block)
            src, dst, dev = m, block_rows + m, prev_dev
        return pltpu.make_async_remote_copy(
            src_ref=strip.at[src, :, cut],
            dst_ref=strip.at[dst, :, cut],
            send_sem=halo_send.at[way, m],
            recv_sem=halo_recv.at[way, m],
            device_id=dev,
            device_id_type=MESH,
        )

    place(0)

    @pl.when(has_next)
    def _():
        for m in range(width):
            halo(0, m).start()

    @pl.when(has_prev)
    def _():
        for m in range(width):
            halo(1, m).start()

    place(1)

    @pl.when(has_prev)
    def _():
        for m in range(width):
            halo(0, m).wait_recv()

    def products(r):
        flags = kept[pl.ds(r, 1), :]
        for e in range(width + 1):
            value = lax.dot_general(
                strip[r, :, e * block :],
                strip[r + e, :, : (2 * width + 1 - e) * block],
                (((1,), (1,)), ((), ())),
                preferred_element_type=jnp.float32,
            )
            if e > 0:
                value = jnp.where(flags[:, e - 1 : e] == 1, value, 0.0)
            prod[r, e] = value.astype(prod.dtype)
        place_row = pos * block_rows + r
        pltpu.make_async_copy(prod.at[r, :, mine, :], out.at[place_row], loc_sem.at[3]).start()

        @pl.loop(1, cols_n)
        def _(k):
            dst = other(k)
            pltpu.make_async_remote_copy(
                src_ref=prod.at[r, :, slab_of(dst), :],
                dst_ref=out.at[place_row],
                send_sem=out_send.at[dst],
                recv_sem=out_recv.at[col],
                device_id=(row, dst),
                device_id_type=MESH,
            ).start()

    products(0)
    place(2)

    @pl.when(has_next)
    def _():
        for m in range(width):
            halo(1, m).wait_recv()

    for d in range(1, width):

        @pl.loop(block_rows, block_rows + width - d)
        def _(r):
            strip[r + d, :, part_of(width - d)] = strip[r, :, part_of(width + d)].T

    pl.loop(1, block_rows)(products)

    @pl.when(has_next)
    def _():
        for m in range(width):
            halo(0, m).wait_send()

    @pl.when(has_prev)
    def _():
        for m in range(width):
            halo(1, m).wait_send()

    def rows_of(c):
        return pl.ds(turned(c) * block_rows, block_rows)

    whole = out.at[rows_of(col)]
    pltpu.make_async_copy(whole, whole, loc_sem.at[3]).wait()

    @pl.loop(1, cols_n)
    def _(k):
        dev = other(k)
        sent = up.at[rows_of(dev)]
        pltpu.make_async_copy(sent, sent, in_send.at[dev]).wait()
        left = prod.at[:, :, slab_of(dev), :]
        pltpu.make_async_copy(left, left, out_send.at[dev]).wait()
        came = out.at[rows_of(dev)]
        pltpu.make_async_copy(came, came, out_recv.at[dev]).wait()


def shards(rows_n, cols_n, upper_tiles, occupied):
    block_rows, width = occupied.shape
    block = upper_tiles.shape[3]
    flags = jnp.pad(occupied, ((0, 0), (0, 128 - width)))
    dma = pltpu.SemaphoreType.DMA
    return pl.pallas_call(
        functools.partial(band_square_kernel, rows_n, cols_n, width),
        out_shape=jax.ShapeDtypeStruct(upper_tiles.shape, upper_tiles.dtype),
        in_specs=[pl.BlockSpec(memory_space=pl.ANY)] * 2,
        out_specs=pl.BlockSpec(memory_space=pl.ANY),
        scratch_shapes=[
            pltpu.VMEM((block_rows, width + 1, block, block), jnp.bfloat16),
            pltpu.VMEM((block_rows + width, block, (2 * width + 1) * block), jnp.bfloat16),
            pltpu.VMEM((block_rows, width + 1, block, block), jnp.bfloat16),
            pltpu.VMEM((block_rows, 128), jnp.int32),
            pltpu.VMEM((block_rows, 128), jnp.int32),
            dma((cols_n,)),
            dma((3, cols_n)),
            dma((2, width)),
            dma((2, width)),
            dma((cols_n,)),
            dma((cols_n,)),
            dma((2,)),
            dma((4,)),
        ],
        compiler_params=pltpu.CompilerParams(
            collective_id=0, has_side_effects=True, vmem_limit_bytes=48 * 2**20
        ),
        cost_estimate=pl.CostEstimate(
            flops=2 * 35 * block_rows * block**3, bytes_accessed=2 * upper_tiles.size * 2, transcendentals=0
        ),
    )(upper_tiles, flags)


def solution(mesh):
    return jax.shard_map(
        functools.partial(shards, mesh.shape["row"], mesh.shape["col"]),
        mesh=mesh,
        in_specs=(P("row", None, "col", None), P(("row", "col"), None)),
        out_specs=P("row", None, "col", None),
        check_vma=False,
    )
```

```python
import functools

import jax
import jax.numpy as jnp
from jax import lax
from jax.experimental import pallas as pl
from jax.experimental.pallas import tpu as pltpu
from jax.sharding import PartitionSpec as P

MESH = pl.DeviceIdType.MESH


def band_square_kernel(
    rows_n,
    cols_n,
    width,
    up,
    occ,
    out,
    tiles,
    strip,
    prod,
    occ_v,
    kept,
    in_send,
    in_recv,
    halo_send,
    halo_recv,
    out_send,
    out_recv,
    occ_sem,
    loc_sem,
):
    block_rows, block = tiles.shape[0], tiles.shape[2]
    slab = block // cols_n
    row, col = lax.axis_index("row"), lax.axis_index("col")
    odd = lax.rem(row, 2)

    def turned(c):
        return jnp.where(odd == 1, cols_n - 1 - c, c)

    pos = turned(col)
    chunk = row * cols_n + pos
    step = 1 - 2 * odd
    has_next, has_prev = chunk < rows_n * cols_n - 1, chunk > 0
    next_out, prev_out = pos == cols_n - 1, pos == 0
    next_dev = (jnp.where(next_out, row + 1, row), jnp.where(next_out, col, col + step))
    prev_dev = (jnp.where(prev_out, row - 1, row), jnp.where(prev_out, col, col - step))

    def other(k):
        return lax.rem(col + k, cols_n)

    barrier = pltpu.get_barrier_semaphore()

    @pl.loop(1, cols_n)
    def _(k):
        pl.semaphore_signal(barrier, inc=1, device_id=(row, other(k)), device_id_type=MESH)

    @pl.when(next_out & has_next)
    def _():
        pl.semaphore_signal(barrier, inc=1, device_id=next_dev, device_id_type=MESH)

    @pl.when(prev_out & has_prev)
    def _():
        pl.semaphore_signal(barrier, inc=1, device_id=prev_dev, device_id_type=MESH)

    outside = (next_out & has_next) | (prev_out & has_prev)
    pl.semaphore_wait(barrier, cols_n - 1 + jnp.where(outside, 1, 0))

    def slab_of(c):
        return pl.ds(pl.multiple_of(c * slab, slab), slab)

    def cells(stage):
        for r in range(block_rows):
            cut = width - r if r < width else block_rows - r
            first, rest = (0, cut), (cut, width + 1)
            if r >= width:
                first, rest = rest, first
            if stage == 0:
                yield r, first
            elif (stage == 1) == (r <= width):
                yield r, rest

    def piece_of(stage, c):
        count = sum(hi - lo for _, (lo, hi) in cells(stage))
        deep = max(n for n in range(1, width + 2) if count % n == 0 and count // n <= block_rows)
        return tiles.at[: count // deep, :deep, slab_of(c), :]

    mine = slab_of(col)
    def send(stage):
        for r, (lo, hi) in cells(stage):
            pltpu.make_async_copy(
                up.at[pos * block_rows + r, lo:hi], tiles.at[r, lo:hi, mine, :], loc_sem.at[stage]
            ).start()

            @pl.loop(1, cols_n)
            def _(k):
                dst = other(k)
                pltpu.make_async_remote_copy(
                    src_ref=up.at[turned(dst) * block_rows + r, lo:hi],
                    dst_ref=tiles.at[r, lo:hi, mine, :],
                    send_sem=in_send.at[dst],
                    recv_sem=in_recv.at[stage, col],
                    device_id=(row, dst),
                    device_id_type=MESH,
                ).start()

    send(0)
    send(1)

    partner = cols_n - 1 - col
    occ_copy = pltpu.make_async_remote_copy(
        src_ref=occ,
        dst_ref=occ_v,
        send_sem=occ_sem.at[0],
        recv_sem=occ_sem.at[1],
        device_id=(row, partner),
        device_id_type=MESH,
    )

    @pl.when(odd == 1)
    def _():
        occ_copy.start()
        occ_copy.wait()

    @pl.when(odd == 0)
    def _():
        here = pltpu.make_async_copy(occ, occ_v, occ_sem.at[1])
        here.start()
        here.wait()

    shape = occ_v.shape
    index = (
        chunk * block_rows
        + lax.broadcasted_iota(jnp.int32, shape, 0)
        + lax.broadcasted_iota(jnp.int32, shape, 1)
        + 1
    )
    total = rows_n * cols_n * block_rows
    kept[...] = jnp.where((occ_v[...] == 1) & (index < total), 1, 0)

    def part_of(n):
        return slice(n * block, (n + 1) * block)

    @pl.when(jnp.logical_not(has_prev))
    def _():
        for q in range(width):
            strip[q, :, : (width - q) * block] = jnp.zeros(
                (block, (width - q) * block), strip.dtype
            )

    @pl.when(jnp.logical_not(has_next))
    def _():
        for m in range(width):
            strip[block_rows + m, :, width * block : (2 * width - m) * block] = jnp.zeros(
                (block, (width - m) * block), strip.dtype
            )

    def arrive(stage):
        piece = piece_of(stage, col)
        pltpu.make_async_copy(piece, piece, loc_sem.at[stage]).wait()

        @pl.loop(1, cols_n)
        def _(k):
            src = other(k)
            piece = piece_of(stage, src)
            pltpu.make_async_copy(piece, piece, in_recv.at[stage, src]).wait()

    def place(stage):
        for d in range(width + 1):
            if stage == 0:
                lo, hi = block_rows - d, block_rows - d + width
            elif stage == 1:
                lo, hi = width - d, min(width + 1, block_rows - d)
            else:
                lo, hi = width + 1, block_rows - d
            if lo >= hi:
                continue

            @pl.loop(lo, hi)
            def _(j):
                r = lax.rem(j, block_rows)
                tile = tiles[r, d]
                if d == 0:
                    full = tile.astype(jnp.float32)
                    strip[r, :, part_of(width)] = (0.5 * (full + full.T)).astype(strip.dtype)
                else:
                    flag = kept[pl.ds(r, 1), :][:, d - 1 : d]
                    tile = jnp.where(flag == 1, tile, jnp.zeros_like(tile))
                    strip[r, :, part_of(width + d)] = tile
                    strip[r + d, :, part_of(width - d)] = tile.T

    def halo(way, m):
        if way == 0:
            cut = slice(0, (width - m) * block)
            src, dst, dev = block_rows + m, m, next_dev
        else:
            cut = slice(width * block, (2 * width - m) * block)
            src, dst, dev = m, block_rows + m, prev_dev
        return pltpu.make_async_remote_copy(
            src_ref=strip.at[src, :, cut],
            dst_ref=strip.at[dst, :, cut],
            send_sem=halo_send.at[way, m],
            recv_sem=halo_recv.at[way, m],
            device_id=dev,
            device_id_type=MESH,
        )

    arrive(0)
    send(2)
    place(0)

    @pl.when(has_next)
    def _():
        for m in range(width):
            halo(0, m).start()

    @pl.when(has_prev)
    def _():
        for m in range(width):
            halo(1, m).start()

    arrive(1)
    place(1)

    @pl.when(has_prev)
    def _():
        for m in range(width):
            halo(0, m).wait_recv()

    def products(r):
        flags = kept[pl.ds(r, 1), :]
        for e in range(width + 1):
            value = lax.dot_general(
                strip[r, :, e * block :],
                strip[r + e, :, : (2 * width + 1 - e) * block],
                (((1,), (1,)), ((), ())),
                preferred_element_type=jnp.float32,
            )
            if e > 0:
                value = jnp.where(flags[:, e - 1 : e] == 1, value, 0.0)
            prod[r, e] = value.astype(prod.dtype)
        place_row = pos * block_rows + r
        pltpu.make_async_copy(prod.at[r, :, mine, :], out.at[place_row], loc_sem.at[3]).start()

        @pl.loop(1, cols_n)
        def _(k):
            dst = other(k)
            pltpu.make_async_remote_copy(
                src_ref=prod.at[r, :, slab_of(dst), :],
                dst_ref=out.at[place_row],
                send_sem=out_send.at[dst],
                recv_sem=out_recv.at[col],
                device_id=(row, dst),
                device_id_type=MESH,
            ).start()

    products(0)
    arrive(2)
    place(2)

    @pl.when(has_next)
    def _():
        for m in range(width):
            halo(1, m).wait_recv()

    for d in range(1, width):

        @pl.loop(block_rows, block_rows + width - d)
        def _(r):
            strip[r + d, :, part_of(width - d)] = strip[r, :, part_of(width + d)].T

    pl.loop(1, block_rows)(products)

    @pl.when(has_next)
    def _():
        for m in range(width):
            halo(0, m).wait_send()

    @pl.when(has_prev)
    def _():
        for m in range(width):
            halo(1, m).wait_send()

    def rows_of(c):
        return pl.ds(turned(c) * block_rows, block_rows)

    whole = out.at[rows_of(col)]
    pltpu.make_async_copy(whole, whole, loc_sem.at[3]).wait()

    @pl.loop(1, cols_n)
    def _(k):
        dev = other(k)
        sent = up.at[rows_of(dev)]
        pltpu.make_async_copy(sent, sent, in_send.at[dev]).wait()
        left = prod.at[:, :, slab_of(dev), :]
        pltpu.make_async_copy(left, left, out_send.at[dev]).wait()
        came = out.at[rows_of(dev)]
        pltpu.make_async_copy(came, came, out_recv.at[dev]).wait()


def shards(rows_n, cols_n, upper_tiles, occupied):
    block_rows, width = occupied.shape
    block = upper_tiles.shape[3]
    flags = jnp.pad(occupied, ((0, 0), (0, 128 - width)))
    dma = pltpu.SemaphoreType.DMA
    return pl.pallas_call(
        functools.partial(band_square_kernel, rows_n, cols_n, width),
        out_shape=jax.ShapeDtypeStruct(upper_tiles.shape, upper_tiles.dtype),
        in_specs=[pl.BlockSpec(memory_space=pl.ANY)] * 2,
        out_specs=pl.BlockSpec(memory_space=pl.ANY),
        scratch_shapes=[
            pltpu.VMEM((block_rows, width + 1, block, block), jnp.bfloat16),
            pltpu.VMEM((block_rows + width, block, (2 * width + 1) * block), jnp.bfloat16),
            pltpu.VMEM((block_rows, width + 1, block, block), jnp.bfloat16),
            pltpu.VMEM((block_rows, 128), jnp.int32),
            pltpu.VMEM((block_rows, 128), jnp.int32),
            dma((cols_n,)),
            dma((3, cols_n)),
            dma((2, width)),
            dma((2, width)),
            dma((cols_n,)),
            dma((cols_n,)),
            dma((2,)),
            dma((4,)),
        ],
        compiler_params=pltpu.CompilerParams(
            collective_id=0, has_side_effects=True, vmem_limit_bytes=48 * 2**20
        ),
        cost_estimate=pl.CostEstimate(
            flops=2 * 35 * block_rows * block**3, bytes_accessed=2 * upper_tiles.size * 2, transcendentals=0
        ),
    )(upper_tiles, flags)


def solution(mesh):
    return jax.shard_map(
        functools.partial(shards, mesh.shape["row"], mesh.shape["col"]),
        mesh=mesh,
        in_specs=(P("row", None, "col", None), P(("row", "col"), None)),
        out_specs=P("row", None, "col", None),
        check_vma=False,
    )
```

```python
import functools

import jax
import jax.numpy as jnp
from jax import lax
from jax.experimental import pallas as pl
from jax.experimental.pallas import tpu as pltpu
from jax.sharding import PartitionSpec as P

MESH = pl.DeviceIdType.MESH


def band_square_kernel(
    rows_n,
    cols_n,
    width,
    up,
    occ,
    out,
    tiles,
    strip,
    prod,
    edge,
    occ_here,
    occ_far,
    kept,
    kept_far,
    in_send,
    in_recv,
    halo_send,
    halo_recv,
    edge_send,
    edge_recv,
    out_send,
    out_recv,
    occ_sem,
    loc_sem,
):
    block_rows, block = tiles.shape[0], tiles.shape[2]
    slab = block // cols_n
    row, col = lax.axis_index("row"), lax.axis_index("col")
    odd = lax.rem(row, 2)

    def turned(c):
        return jnp.where(odd == 1, cols_n - 1 - c, c)

    pos = turned(col)
    chunk = row * cols_n + pos
    step = 1 - 2 * odd
    lower, upper = cols_n // 2 - 1, cols_n // 2
    has_next, has_prev = chunk < rows_n * cols_n - 1, chunk > 0
    pass_next, pass_prev = has_next & (pos != lower), has_prev & (pos != upper)
    next_out, prev_out = pos == cols_n - 1, pos == 0
    next_dev = (jnp.where(next_out, row + 1, row), jnp.where(next_out, col, col + step))
    prev_dev = (jnp.where(prev_out, row - 1, row), jnp.where(prev_out, col, col - step))

    def other(k):
        return lax.rem(col + k, cols_n)

    barrier = pltpu.get_barrier_semaphore()

    @pl.loop(1, cols_n)
    def _(k):
        pl.semaphore_signal(barrier, inc=1, device_id=(row, other(k)), device_id_type=MESH)

    @pl.when(next_out & has_next)
    def _():
        pl.semaphore_signal(barrier, inc=1, device_id=next_dev, device_id_type=MESH)

    @pl.when(prev_out & has_prev)
    def _():
        pl.semaphore_signal(barrier, inc=1, device_id=prev_dev, device_id_type=MESH)

    outside = (next_out & has_next) | (prev_out & has_prev)
    pl.semaphore_wait(barrier, cols_n - 1 + jnp.where(outside, 1, 0))

    def slab_of(c):
        return pl.ds(pl.multiple_of(c * slab, slab), slab)

    def cells(stage):
        for r in range(block_rows):
            cut = width - r if r < width else block_rows - r
            first, rest = (0, cut), (cut, width + 1)
            if r >= width:
                first, rest = rest, first
            if stage == 0:
                yield r, first
            elif (stage == 1) == (r <= width):
                yield r, rest

    def piece_of(stage, c):
        count = sum(hi - lo for _, (lo, hi) in cells(stage))
        deep = max(n for n in range(1, width + 2) if count % n == 0 and count // n <= block_rows)
        return tiles.at[: count // deep, :deep, slab_of(c), :]

    mine = slab_of(col)
    def send(stage):
        for r, (lo, hi) in cells(stage):
            pltpu.make_async_copy(
                up.at[pos * block_rows + r, lo:hi], tiles.at[r, lo:hi, mine, :], loc_sem.at[stage]
            ).start()

            @pl.loop(1, cols_n)
            def _(k):
                dst = other(k)
                pltpu.make_async_remote_copy(
                    src_ref=up.at[turned(dst) * block_rows + r, lo:hi],
                    dst_ref=tiles.at[r, lo:hi, mine, :],
                    send_sem=in_send.at[dst],
                    recv_sem=in_recv.at[stage, col],
                    device_id=(row, dst),
                    device_id_type=MESH,
                ).start()

    def edge_span(way, m):
        return (lower * block_rows + width + m, width - m, m + 1) if way == 0 else (
            upper * block_rows + m, 0, width - m)

    edge_to = (turned(upper), turned(lower))

    def send_edge(way):
        for m in range(width):
            r, lo, count = edge_span(way, m)
            src, dst = up.at[r, lo : lo + count], edge.at[m, :count, mine, :]

            @pl.when(col != edge_to[way])
            def _():
                pltpu.make_async_remote_copy(
                    src_ref=src,
                    dst_ref=dst,
                    send_sem=edge_send.at[way],
                    recv_sem=edge_recv.at[col],
                    device_id=(row, edge_to[way]),
                    device_id_type=MESH,
                ).start()

            @pl.when(col == edge_to[way])
            def _():
                pltpu.make_async_copy(src, dst, edge_recv.at[col]).start()

    def edge_piece(c):
        return tiles.at[: width // 2, : width + 1, slab_of(c), :]

    def arrive_edge():
        @pl.loop(0, cols_n)
        def _(c):
            piece = edge_piece(c)
            pltpu.make_async_copy(piece, piece, edge_recv.at[c]).wait()

    send(0)
    send_edge(0)
    send_edge(1)
    send(1)

    partner = cols_n - 1 - col
    occ_copy = pltpu.make_async_remote_copy(
        src_ref=occ,
        dst_ref=occ_far,
        send_sem=occ_sem.at[0],
        recv_sem=occ_sem.at[1],
        device_id=(row, partner),
        device_id_type=MESH,
    )
    occ_copy.start()
    occ_local = pltpu.make_async_copy(occ, occ_here, occ_sem.at[2])
    occ_local.start()
    occ_local.wait()
    occ_copy.wait()

    shape = kept.shape
    offset = (
        lax.broadcasted_iota(jnp.int32, shape, 0) + lax.broadcasted_iota(jnp.int32, shape, 1) + 1
    )
    total = rows_n * cols_n * block_rows
    chunk_far = row * cols_n + cols_n - 1 - pos
    flags_here, flags_far = occ_here[...], occ_far[...]
    for ref, flags, number in (
        (kept, jnp.where(odd == 1, flags_far, flags_here), chunk),
        (kept_far, jnp.where(odd == 1, flags_here, flags_far), chunk_far),
    ):
        ref[...] = jnp.where((flags == 1) & (number * block_rows + offset < total), 1, 0)

    def part_of(n):
        return slice(n * block, (n + 1) * block)

    @pl.when(jnp.logical_not(has_prev))
    def _():
        for q in range(width):
            strip[q, :, : (width - q) * block] = jnp.zeros(
                (block, (width - q) * block), strip.dtype
            )

    @pl.when(jnp.logical_not(has_next))
    def _():
        for m in range(width):
            strip[block_rows + m, :, width * block : (2 * width - m) * block] = jnp.zeros(
                (block, (width - m) * block), strip.dtype
            )

    def arrive(stage):
        piece = piece_of(stage, col)
        pltpu.make_async_copy(piece, piece, loc_sem.at[stage]).wait()

        @pl.loop(1, cols_n)
        def _(k):
            src = other(k)
            piece = piece_of(stage, src)
            pltpu.make_async_copy(piece, piece, in_recv.at[stage, src]).wait()

    def place(stage):
        for d in range(width + 1):
            if stage == 0:
                lo, hi = block_rows - d, block_rows - d + width
            elif stage == 1:
                lo, hi = width - d, min(width + 1, block_rows - d)
            else:
                lo, hi = width + 1, block_rows - d
            if lo >= hi:
                continue

            @pl.loop(lo, hi)
            def _(j):
                r = lax.rem(j, block_rows)
                tile = tiles[r, d]
                if d == 0:
                    strip[r, :, part_of(width)] = symmetric(tile)
                else:
                    tile = masked(tile, kept[pl.ds(r, 1), :], d)
                    strip[r, :, part_of(width + d)] = tile
                    strip[r + d, :, part_of(width - d)] = tile.T

    def masked(tile, flags, d):
        return jnp.where(flags[:, d - 1 : d] == 1, tile, jnp.zeros_like(tile))

    def symmetric(tile):
        full = tile.astype(jnp.float32)
        return (0.5 * (full + full.T)).astype(strip.dtype)

    def place_upper():
        for m in range(width):
            for q in range(m + 1):
                flags = kept_far[width + m : width + m + 1, :]
                tile = masked(edge[m, q], flags, width - m + q)
                strip[q, :, part_of(m - q)] = tile.T

    def place_lower():
        for m in range(width):
            strip[block_rows + m, :, part_of(width)] = symmetric(edge[m, 0])
            for d in range(1, width - m):
                flags = kept_far[m : m + 1, :]
                strip[block_rows + m, :, part_of(width + d)] = masked(edge[m, d], flags, d)

    def halo(way, m):
        if way == 0:
            cut = slice(0, (width - m) * block)
            src, dst, dev = block_rows + m, m, next_dev
        else:
            cut = slice(width * block, (2 * width - m) * block)
            src, dst, dev = m, block_rows + m, prev_dev
        return pltpu.make_async_remote_copy(
            src_ref=strip.at[src, :, cut],
            dst_ref=strip.at[dst, :, cut],
            send_sem=halo_send.at[way, m],
            recv_sem=halo_recv.at[way, m],
            device_id=dev,
            device_id_type=MESH,
        )

    arrive(0)
    send(2)
    place(0)

    @pl.when(pass_next)
    def _():
        for m in range(width):
            halo(0, m).start()

    @pl.when(pass_prev)
    def _():
        for m in range(width):
            halo(1, m).start()

    arrive(1)
    place(1)

    @pl.when(pass_prev)
    def _():
        for m in range(width):
            halo(0, m).wait_recv()

    @pl.when(pos == upper)
    def _():
        arrive_edge()
        place_upper()

    def products(r):
        flags = kept[pl.ds(r, 1), :]
        for e in range(width + 1):
            value = lax.dot_general(
                strip[r, :, e * block :],
                strip[r + e, :, : (2 * width + 1 - e) * block],
                (((1,), (1,)), ((), ())),
                preferred_element_type=jnp.float32,
            )
            if e > 0:
                value = jnp.where(flags[:, e - 1 : e] == 1, value, 0.0)
            prod[r, e] = value.astype(prod.dtype)
        place_row = pos * block_rows + r
        pltpu.make_async_copy(prod.at[r, :, mine, :], out.at[place_row], loc_sem.at[3]).start()

        @pl.loop(1, cols_n)
        def _(k):
            dst = other(k)
            pltpu.make_async_remote_copy(
                src_ref=prod.at[r, :, slab_of(dst), :],
                dst_ref=out.at[place_row],
                send_sem=out_send.at[dst],
                recv_sem=out_recv.at[col],
                device_id=(row, dst),
                device_id_type=MESH,
            ).start()

    products(0)
    arrive(2)
    place(2)

    @pl.when(pass_next)
    def _():
        for m in range(width):
            halo(1, m).wait_recv()

    @pl.when(pos == lower)
    def _():
        arrive_edge()
        place_lower()

    for d in range(1, width):

        @pl.loop(block_rows, block_rows + width - d)
        def _(r):
            strip[r + d, :, part_of(width - d)] = strip[r, :, part_of(width + d)].T

    pl.loop(1, block_rows)(products)

    @pl.when(pass_next)
    def _():
        for m in range(width):
            halo(0, m).wait_send()

    @pl.when(pass_prev)
    def _():
        for m in range(width):
            halo(1, m).wait_send()

    for way in range(2):

        @pl.when(col != edge_to[way])
        def _():
            piece = edge_piece(col)
            pltpu.make_async_copy(piece, piece, edge_send.at[way]).wait()

    def rows_of(c):
        return pl.ds(turned(c) * block_rows, block_rows)

    whole = out.at[rows_of(col)]
    pltpu.make_async_copy(whole, whole, loc_sem.at[3]).wait()

    @pl.loop(1, cols_n)
    def _(k):
        dev = other(k)
        sent = up.at[rows_of(dev)]
        pltpu.make_async_copy(sent, sent, in_send.at[dev]).wait()
        left = prod.at[:, :, slab_of(dev), :]
        pltpu.make_async_copy(left, left, out_send.at[dev]).wait()
        came = out.at[rows_of(dev)]
        pltpu.make_async_copy(came, came, out_recv.at[dev]).wait()


def shards(rows_n, cols_n, upper_tiles, occupied):
    block_rows, width = occupied.shape
    block = upper_tiles.shape[3]
    flags = jnp.pad(occupied, ((0, 0), (0, 128 - width)))
    dma = pltpu.SemaphoreType.DMA
    return pl.pallas_call(
        functools.partial(band_square_kernel, rows_n, cols_n, width),
        out_shape=jax.ShapeDtypeStruct(upper_tiles.shape, upper_tiles.dtype),
        in_specs=[pl.BlockSpec(memory_space=pl.ANY)] * 2,
        out_specs=pl.BlockSpec(memory_space=pl.ANY),
        scratch_shapes=[
            pltpu.VMEM((block_rows, width + 1, block, block), jnp.bfloat16),
            pltpu.VMEM((block_rows + width, block, (2 * width + 1) * block), jnp.bfloat16),
            pltpu.VMEM((block_rows, width + 1, block, block), jnp.bfloat16),
            pltpu.VMEM((width, width, block, block), jnp.bfloat16),
            pltpu.VMEM((block_rows, 128), jnp.int32),
            pltpu.VMEM((block_rows, 128), jnp.int32),
            pltpu.VMEM((block_rows, 128), jnp.int32),
            pltpu.VMEM((block_rows, 128), jnp.int32),
            dma((cols_n,)),
            dma((3, cols_n)),
            dma((2, width)),
            dma((2, width)),
            dma((2,)),
            dma((cols_n,)),
            dma((cols_n,)),
            dma((cols_n,)),
            dma((3,)),
            dma((4,)),
        ],
        compiler_params=pltpu.CompilerParams(
            collective_id=0, has_side_effects=True, vmem_limit_bytes=48 * 2**20
        ),
        cost_estimate=pl.CostEstimate(
            flops=2 * 35 * block_rows * block**3, bytes_accessed=2 * upper_tiles.size * 2, transcendentals=0
        ),
    )(upper_tiles, flags)


def solution(mesh):
    return jax.shard_map(
        functools.partial(shards, mesh.shape["row"], mesh.shape["col"]),
        mesh=mesh,
        in_specs=(P("row", None, "col", None), P(("row", "col"), None)),
        out_specs=P("row", None, "col", None),
        check_vma=False,
    )
```

```python
import functools

import jax
import jax.numpy as jnp
from jax import lax
from jax.experimental import pallas as pl
from jax.experimental.pallas import tpu as pltpu
from jax.sharding import PartitionSpec as P

MESH = pl.DeviceIdType.MESH


def band_square_kernel(
    rows_n,
    cols_n,
    width,
    up,
    occ,
    out,
    tiles,
    strip,
    prod,
    edge,
    occ_here,
    occ_far,
    kept,
    kept_far,
    in_send,
    in_recv,
    halo_send,
    halo_recv,
    edge_send,
    edge_recv,
    out_send,
    out_recv,
    occ_sem,
    loc_sem,
):
    block_rows, block = tiles.shape[0], tiles.shape[2]
    slab = block // cols_n
    row, col = lax.axis_index("row"), lax.axis_index("col")
    odd = lax.rem(row, 2)

    def turned(c):
        return jnp.where(odd == 1, cols_n - 1 - c, c)

    pos = turned(col)
    chunk = row * cols_n + pos
    step = 1 - 2 * odd
    lower, upper = cols_n // 2 - 1, cols_n // 2
    has_next, has_prev = chunk < rows_n * cols_n - 1, chunk > 0
    pass_next, pass_prev = has_next & (pos != lower), has_prev & (pos != upper)
    next_out, prev_out = pos == cols_n - 1, pos == 0
    next_dev = (jnp.where(next_out, row + 1, row), jnp.where(next_out, col, col + step))
    prev_dev = (jnp.where(prev_out, row - 1, row), jnp.where(prev_out, col, col - step))

    def other(k):
        return lax.rem(col + k, cols_n)

    barrier = pltpu.get_barrier_semaphore()

    @pl.loop(1, cols_n)
    def _(k):
        pl.semaphore_signal(barrier, inc=1, device_id=(row, other(k)), device_id_type=MESH)

    @pl.when(next_out & has_next)
    def _():
        pl.semaphore_signal(barrier, inc=1, device_id=next_dev, device_id_type=MESH)

    @pl.when(prev_out & has_prev)
    def _():
        pl.semaphore_signal(barrier, inc=1, device_id=prev_dev, device_id_type=MESH)

    outside = (next_out & has_next) | (prev_out & has_prev)
    pl.semaphore_wait(barrier, cols_n - 1 + jnp.where(outside, 1, 0))

    def slab_of(c):
        return pl.ds(pl.multiple_of(c * slab, slab), slab)

    def cells(stage):
        for r in range(block_rows):
            cut = width - r if r < width else block_rows - r
            first, rest = (0, cut), (cut, width + 1)
            if r >= width:
                first, rest = rest, first
            if stage == (1 if r < width else 0):
                yield r, first
            elif stage == (2 if r <= width else 3):
                yield r, rest

    def piece_of(stage, c):
        count = sum(hi - lo for _, (lo, hi) in cells(stage))
        deep = max(n for n in range(1, width + 2) if count % n == 0 and count // n <= block_rows)
        return tiles.at[: count // deep, :deep, slab_of(c), :]

    mine = slab_of(col)
    def send(stage):
        for r, (lo, hi) in cells(stage):
            pltpu.make_async_copy(
                up.at[pos * block_rows + r, lo:hi], tiles.at[r, lo:hi, mine, :], loc_sem.at[stage]
            ).start()

            @pl.loop(1, cols_n)
            def _(k):
                dst = other(k)
                pltpu.make_async_remote_copy(
                    src_ref=up.at[turned(dst) * block_rows + r, lo:hi],
                    dst_ref=tiles.at[r, lo:hi, mine, :],
                    send_sem=in_send.at[dst],
                    recv_sem=in_recv.at[stage, col],
                    device_id=(row, dst),
                    device_id_type=MESH,
                ).start()

    def edge_span(way, m):
        return (lower * block_rows + width + m, width - m, m + 1) if way == 0 else (
            upper * block_rows + m, 0, width - m)

    edge_to = (turned(upper), turned(lower))

    def send_edge(way):
        for m in range(width):
            r, lo, count = edge_span(way, m)
            src, dst = up.at[r, lo : lo + count], edge.at[m, :count, mine, :]

            @pl.when(col != edge_to[way])
            def _():
                pltpu.make_async_remote_copy(
                    src_ref=src,
                    dst_ref=dst,
                    send_sem=edge_send.at[way],
                    recv_sem=edge_recv.at[col],
                    device_id=(row, edge_to[way]),
                    device_id_type=MESH,
                ).start()

            @pl.when(col == edge_to[way])
            def _():
                pltpu.make_async_copy(src, dst, edge_recv.at[col]).start()

    def edge_piece(c):
        return tiles.at[: width // 2, : width + 1, slab_of(c), :]

    def arrive_edge():
        @pl.loop(0, cols_n)
        def _(c):
            piece = edge_piece(c)
            pltpu.make_async_copy(piece, piece, edge_recv.at[c]).wait()

    send(0)
    send_edge(0)
    send(1)
    send_edge(1)

    partner = cols_n - 1 - col
    occ_copy = pltpu.make_async_remote_copy(
        src_ref=occ,
        dst_ref=occ_far,
        send_sem=occ_sem.at[0],
        recv_sem=occ_sem.at[1],
        device_id=(row, partner),
        device_id_type=MESH,
    )
    occ_copy.start()
    occ_local = pltpu.make_async_copy(occ, occ_here, occ_sem.at[2])
    occ_local.start()
    occ_local.wait()
    occ_copy.wait()

    shape = kept.shape
    offset = (
        lax.broadcasted_iota(jnp.int32, shape, 0) + lax.broadcasted_iota(jnp.int32, shape, 1) + 1
    )
    total = rows_n * cols_n * block_rows
    chunk_far = row * cols_n + cols_n - 1 - pos
    flags_here, flags_far = occ_here[...], occ_far[...]
    for ref, flags, number in (
        (kept, jnp.where(odd == 1, flags_far, flags_here), chunk),
        (kept_far, jnp.where(odd == 1, flags_here, flags_far), chunk_far),
    ):
        ref[...] = jnp.where((flags == 1) & (number * block_rows + offset < total), 1, 0)

    def part_of(n):
        return slice(n * block, (n + 1) * block)

    @pl.when(jnp.logical_not(has_prev))
    def _():
        for q in range(width):
            strip[q, :, : (width - q) * block] = jnp.zeros(
                (block, (width - q) * block), strip.dtype
            )

    @pl.when(jnp.logical_not(has_next))
    def _():
        for m in range(width):
            strip[block_rows + m, :, width * block : (2 * width - m) * block] = jnp.zeros(
                (block, (width - m) * block), strip.dtype
            )

    def arrive(stage):
        piece = piece_of(stage, col)
        pltpu.make_async_copy(piece, piece, loc_sem.at[stage]).wait()

        @pl.loop(1, cols_n)
        def _(k):
            src = other(k)
            piece = piece_of(stage, src)
            pltpu.make_async_copy(piece, piece, in_recv.at[stage, src]).wait()

    def place(stage):
        for d in range(width + 1):
            lo, hi = (
                (block_rows - d, block_rows),
                (0, width - d),
                (width - d, min(width + 1, block_rows - d)),
                (width + 1, block_rows - d),
            )[stage]
            if lo >= hi:
                continue

            @pl.loop(lo, hi)
            def _(r):
                tile = tiles[r, d]
                if d == 0:
                    strip[r, :, part_of(width)] = symmetric(tile)
                else:
                    tile = masked(tile, kept[pl.ds(r, 1), :], d)
                    strip[r, :, part_of(width + d)] = tile
                    strip[r + d, :, part_of(width - d)] = tile.T

    def masked(tile, flags, d):
        return jnp.where(flags[:, d - 1 : d] == 1, tile, jnp.zeros_like(tile))

    def symmetric(tile):
        full = tile.astype(jnp.float32)
        return (0.5 * (full + full.T)).astype(strip.dtype)

    def place_upper():
        for m in range(width):
            for q in range(m + 1):
                flags = kept_far[width + m : width + m + 1, :]
                tile = masked(edge[m, q], flags, width - m + q)
                strip[q, :, part_of(m - q)] = tile.T

    def place_lower():
        for m in range(width):
            strip[block_rows + m, :, part_of(width)] = symmetric(edge[m, 0])
            for d in range(1, width - m):
                flags = kept_far[m : m + 1, :]
                strip[block_rows + m, :, part_of(width + d)] = masked(edge[m, d], flags, d)

    def halo(way, m):
        if way == 0:
            cut = slice(0, (width - m) * block)
            src, dst, dev = block_rows + m, m, next_dev
        else:
            cut = slice(width * block, (2 * width - m) * block)
            src, dst, dev = m, block_rows + m, prev_dev
        return pltpu.make_async_remote_copy(
            src_ref=strip.at[src, :, cut],
            dst_ref=strip.at[dst, :, cut],
            send_sem=halo_send.at[way, m],
            recv_sem=halo_recv.at[way, m],
            device_id=dev,
            device_id_type=MESH,
        )

    arrive(0)
    send(2)
    place(0)

    @pl.when(pass_next)
    def _():
        for m in range(width):
            halo(0, m).start()

    arrive(1)
    send(3)
    place(1)

    @pl.when(pass_prev)
    def _():
        for m in range(width):
            halo(1, m).start()

    arrive(2)
    place(2)

    @pl.when(pass_prev)
    def _():
        for m in range(width):
            halo(0, m).wait_recv()

    @pl.when(pos == upper)
    def _():
        arrive_edge()
        place_upper()

    def products(r):
        flags = kept[pl.ds(r, 1), :]
        for e in range(width + 1):
            value = lax.dot_general(
                strip[r, :, e * block :],
                strip[r + e, :, : (2 * width + 1 - e) * block],
                (((1,), (1,)), ((), ())),
                preferred_element_type=jnp.float32,
            )
            if e > 0:
                value = jnp.where(flags[:, e - 1 : e] == 1, value, 0.0)
            prod[r, e] = value.astype(prod.dtype)
        place_row = pos * block_rows + r
        pltpu.make_async_copy(prod.at[r, :, mine, :], out.at[place_row], loc_sem.at[4]).start()

        @pl.loop(1, cols_n)
        def _(k):
            dst = other(k)
            pltpu.make_async_remote_copy(
                src_ref=prod.at[r, :, slab_of(dst), :],
                dst_ref=out.at[place_row],
                send_sem=out_send.at[dst],
                recv_sem=out_recv.at[col],
                device_id=(row, dst),
                device_id_type=MESH,
            ).start()

    products(0)
    arrive(3)
    place(3)

    @pl.when(pass_next)
    def _():
        for m in range(width):
            halo(1, m).wait_recv()

    @pl.when(pos == lower)
    def _():
        arrive_edge()
        place_lower()

    for d in range(1, width):

        @pl.loop(block_rows, block_rows + width - d)
        def _(r):
            strip[r + d, :, part_of(width - d)] = strip[r, :, part_of(width + d)].T

    pl.loop(1, block_rows)(products)

    @pl.when(pass_next)
    def _():
        for m in range(width):
            halo(0, m).wait_send()

    @pl.when(pass_prev)
    def _():
        for m in range(width):
            halo(1, m).wait_send()

    for way in range(2):

        @pl.when(col != edge_to[way])
        def _():
            piece = edge_piece(col)
            pltpu.make_async_copy(piece, piece, edge_send.at[way]).wait()

    def rows_of(c):
        return pl.ds(turned(c) * block_rows, block_rows)

    whole = out.at[rows_of(col)]
    pltpu.make_async_copy(whole, whole, loc_sem.at[4]).wait()

    @pl.loop(1, cols_n)
    def _(k):
        dev = other(k)
        sent = up.at[rows_of(dev)]
        pltpu.make_async_copy(sent, sent, in_send.at[dev]).wait()
        left = prod.at[:, :, slab_of(dev), :]
        pltpu.make_async_copy(left, left, out_send.at[dev]).wait()
        came = out.at[rows_of(dev)]
        pltpu.make_async_copy(came, came, out_recv.at[dev]).wait()


def shards(rows_n, cols_n, upper_tiles, occupied):
    block_rows, width = occupied.shape
    block = upper_tiles.shape[3]
    flags = jnp.pad(occupied, ((0, 0), (0, 128 - width)))
    dma = pltpu.SemaphoreType.DMA
    return pl.pallas_call(
        functools.partial(band_square_kernel, rows_n, cols_n, width),
        out_shape=jax.ShapeDtypeStruct(upper_tiles.shape, upper_tiles.dtype),
        in_specs=[pl.BlockSpec(memory_space=pl.ANY)] * 2,
        out_specs=pl.BlockSpec(memory_space=pl.ANY),
        scratch_shapes=[
            pltpu.VMEM((block_rows, width + 1, block, block), jnp.bfloat16),
            pltpu.VMEM((block_rows + width, block, (2 * width + 1) * block), jnp.bfloat16),
            pltpu.VMEM((block_rows, width + 1, block, block), jnp.bfloat16),
            pltpu.VMEM((width, width, block, block), jnp.bfloat16),
            pltpu.VMEM((block_rows, 128), jnp.int32),
            pltpu.VMEM((block_rows, 128), jnp.int32),
            pltpu.VMEM((block_rows, 128), jnp.int32),
            pltpu.VMEM((block_rows, 128), jnp.int32),
            dma((cols_n,)),
            dma((4, cols_n)),
            dma((2, width)),
            dma((2, width)),
            dma((2,)),
            dma((cols_n,)),
            dma((cols_n,)),
            dma((cols_n,)),
            dma((3,)),
            dma((5,)),
        ],
        compiler_params=pltpu.CompilerParams(
            collective_id=0, has_side_effects=True, vmem_limit_bytes=48 * 2**20
        ),
        cost_estimate=pl.CostEstimate(
            flops=2 * 35 * block_rows * block**3, bytes_accessed=2 * upper_tiles.size * 2, transcendentals=0
        ),
    )(upper_tiles, flags)


def solution(mesh):
    return jax.shard_map(
        functools.partial(shards, mesh.shape["row"], mesh.shape["col"]),
        mesh=mesh,
        in_specs=(P("row", None, "col", None), P(("row", "col"), None)),
        out_specs=P("row", None, "col", None),
        check_vma=False,
    )
```

```python
import functools

import jax
import jax.numpy as jnp
from jax import lax
from jax.experimental import pallas as pl
from jax.experimental.pallas import tpu as pltpu
from jax.sharding import PartitionSpec as P

MESH = pl.DeviceIdType.MESH


def band_square_kernel(
    rows_n,
    cols_n,
    width,
    up,
    occ,
    out,
    tiles,
    strip,
    prod,
    edge,
    occ_here,
    occ_far,
    kept,
    kept_far,
    in_send,
    in_recv,
    halo_send,
    halo_recv,
    edge_send,
    edge_recv,
    out_send,
    out_recv,
    occ_sem,
    loc_sem,
):
    block_rows, block = tiles.shape[0], tiles.shape[2]
    slab = block // cols_n
    row, col = lax.axis_index("row"), lax.axis_index("col")
    odd = lax.rem(row, 2)

    def turned(c):
        return jnp.where(odd == 1, cols_n - 1 - c, c)

    pos = turned(col)
    chunk = row * cols_n + pos
    step = 1 - 2 * odd
    lower, upper = cols_n // 2 - 1, cols_n // 2
    has_next, has_prev = chunk < rows_n * cols_n - 1, chunk > 0
    pass_next, pass_prev = has_next & (pos != lower), has_prev & (pos != upper)
    next_out, prev_out = pos == cols_n - 1, pos == 0
    next_dev = (jnp.where(next_out, row + 1, row), jnp.where(next_out, col, col + step))
    prev_dev = (jnp.where(prev_out, row - 1, row), jnp.where(prev_out, col, col - step))

    def other(k):
        return lax.rem(col + k, cols_n)

    half = cols_n // 2
    inside, base = lax.rem(col, half), col // half * half

    def target(k):
        step = jnp.where(k < half, k, k - half + 1)
        return jnp.where(k < half, half - base, base) + lax.rem(inside + step, half)

    barrier = pltpu.get_barrier_semaphore()

    @pl.loop(1, cols_n)
    def _(k):
        pl.semaphore_signal(barrier, inc=1, device_id=(row, other(k)), device_id_type=MESH)

    @pl.when(next_out & has_next)
    def _():
        pl.semaphore_signal(barrier, inc=1, device_id=next_dev, device_id_type=MESH)

    @pl.when(prev_out & has_prev)
    def _():
        pl.semaphore_signal(barrier, inc=1, device_id=prev_dev, device_id_type=MESH)

    outside = (next_out & has_next) | (prev_out & has_prev)
    pl.semaphore_wait(barrier, cols_n - 1 + jnp.where(outside, 1, 0))

    def slab_of(c):
        return pl.ds(pl.multiple_of(c * slab, slab), slab)

    def cells(stage):
        for r in range(block_rows):
            cut = width - r if r < width else block_rows - r
            first, rest = (0, cut), (cut, width + 1)
            if r >= width:
                first, rest = rest, first
            if stage == 0:
                yield r, first
            elif (stage == 1) == (r <= width):
                yield r, rest

    def piece_of(stage, c):
        count = sum(hi - lo for _, (lo, hi) in cells(stage))
        deep = max(n for n in range(1, width + 2) if count % n == 0 and count // n <= block_rows)
        return tiles.at[: count // deep, :deep, slab_of(c), :]

    mine = slab_of(col)
    def send(stage):
        for r, (lo, hi) in cells(stage):
            pltpu.make_async_copy(
                up.at[pos * block_rows + r, lo:hi], tiles.at[r, lo:hi, mine, :], loc_sem.at[stage]
            ).start()

            @pl.loop(0, cols_n - 1)
            def _(k):
                dst = target(k)
                pltpu.make_async_remote_copy(
                    src_ref=up.at[turned(dst) * block_rows + r, lo:hi],
                    dst_ref=tiles.at[r, lo:hi, mine, :],
                    send_sem=in_send.at[dst],
                    recv_sem=in_recv.at[stage, col],
                    device_id=(row, dst),
                    device_id_type=MESH,
                ).start()

    def edge_span(way, m):
        return (lower * block_rows + width + m, width - m, m + 1) if way == 0 else (
            upper * block_rows + m, 0, width - m)

    edge_to = (turned(upper), turned(lower))

    def send_edge(way):
        for m in range(width):
            r, lo, count = edge_span(way, m)
            src, dst = up.at[r, lo : lo + count], edge.at[m, :count, mine, :]

            @pl.when(col != edge_to[way])
            def _():
                pltpu.make_async_remote_copy(
                    src_ref=src,
                    dst_ref=dst,
                    send_sem=edge_send.at[way],
                    recv_sem=edge_recv.at[col],
                    device_id=(row, edge_to[way]),
                    device_id_type=MESH,
                ).start()

            @pl.when(col == edge_to[way])
            def _():
                pltpu.make_async_copy(src, dst, edge_recv.at[col]).start()

    def edge_piece(c):
        return tiles.at[: width // 2, : width + 1, slab_of(c), :]

    def arrive_edge():
        @pl.loop(0, cols_n)
        def _(c):
            piece = edge_piece(c)
            pltpu.make_async_copy(piece, piece, edge_recv.at[c]).wait()

    send(0)
    send_edge(0)
    send_edge(1)
    send(1)

    partner = cols_n - 1 - col
    occ_copy = pltpu.make_async_remote_copy(
        src_ref=occ,
        dst_ref=occ_far,
        send_sem=occ_sem.at[0],
        recv_sem=occ_sem.at[1],
        device_id=(row, partner),
        device_id_type=MESH,
    )
    occ_copy.start()
    occ_local = pltpu.make_async_copy(occ, occ_here, occ_sem.at[2])
    occ_local.start()
    occ_local.wait()
    occ_copy.wait()

    shape = kept.shape
    offset = (
        lax.broadcasted_iota(jnp.int32, shape, 0) + lax.broadcasted_iota(jnp.int32, shape, 1) + 1
    )
    total = rows_n * cols_n * block_rows
    chunk_far = row * cols_n + cols_n - 1 - pos
    flags_here, flags_far = occ_here[...], occ_far[...]
    for ref, flags, number in (
        (kept, jnp.where(odd == 1, flags_far, flags_here), chunk),
        (kept_far, jnp.where(odd == 1, flags_here, flags_far), chunk_far),
    ):
        ref[...] = jnp.where((flags == 1) & (number * block_rows + offset < total), 1, 0)

    def part_of(n):
        return slice(n * block, (n + 1) * block)

    @pl.when(jnp.logical_not(has_prev))
    def _():
        for q in range(width):
            strip[q, :, : (width - q) * block] = jnp.zeros(
                (block, (width - q) * block), strip.dtype
            )

    @pl.when(jnp.logical_not(has_next))
    def _():
        for m in range(width):
            strip[block_rows + m, :, width * block : (2 * width - m) * block] = jnp.zeros(
                (block, (width - m) * block), strip.dtype
            )

    def arrive(stage):
        piece = piece_of(stage, col)
        pltpu.make_async_copy(piece, piece, loc_sem.at[stage]).wait()

        @pl.loop(1, cols_n)
        def _(k):
            src = other(k)
            piece = piece_of(stage, src)
            pltpu.make_async_copy(piece, piece, in_recv.at[stage, src]).wait()

    def place(stage):
        for d in range(width + 1):
            if stage == 0:
                lo, hi = block_rows - d, block_rows - d + width
            elif stage == 1:
                lo, hi = width - d, min(width + 1, block_rows - d)
            else:
                lo, hi = width + 1, block_rows - d
            if lo >= hi:
                continue

            @pl.loop(lo, hi)
            def _(j):
                r = lax.rem(j, block_rows)
                tile = tiles[r, d]
                if d == 0:
                    strip[r, :, part_of(width)] = symmetric(tile)
                else:
                    tile = masked(tile, kept[pl.ds(r, 1), :], d)
                    strip[r, :, part_of(width + d)] = tile
                    strip[r + d, :, part_of(width - d)] = tile.T

    def masked(tile, flags, d):
        return jnp.where(flags[:, d - 1 : d] == 1, tile, jnp.zeros_like(tile))

    def symmetric(tile):
        full = tile.astype(jnp.float32)
        return (0.5 * (full + full.T)).astype(strip.dtype)

    def place_upper():
        for m in range(width):
            for q in range(m + 1):
                flags = kept_far[width + m : width + m + 1, :]
                tile = masked(edge[m, q], flags, width - m + q)
                strip[q, :, part_of(m - q)] = tile.T

    def place_lower():
        for m in range(width):
            strip[block_rows + m, :, part_of(width)] = symmetric(edge[m, 0])
            for d in range(1, width - m):
                flags = kept_far[m : m + 1, :]
                strip[block_rows + m, :, part_of(width + d)] = masked(edge[m, d], flags, d)

    def halo(way, m):
        if way == 0:
            cut = slice(0, (width - m) * block)
            src, dst, dev = block_rows + m, m, next_dev
        else:
            cut = slice(width * block, (2 * width - m) * block)
            src, dst, dev = m, block_rows + m, prev_dev
        return pltpu.make_async_remote_copy(
            src_ref=strip.at[src, :, cut],
            dst_ref=strip.at[dst, :, cut],
            send_sem=halo_send.at[way, m],
            recv_sem=halo_recv.at[way, m],
            device_id=dev,
            device_id_type=MESH,
        )

    arrive(0)
    send(2)
    place(0)

    @pl.when(pass_next)
    def _():
        for m in range(width):
            halo(0, m).start()

    @pl.when(pass_prev)
    def _():
        for m in range(width):
            halo(1, m).start()

    arrive(1)
    place(1)

    @pl.when(pass_prev)
    def _():
        for m in range(width):
            halo(0, m).wait_recv()

    @pl.when(pos == upper)
    def _():
        arrive_edge()
        place_upper()

    def products(r):
        flags = kept[pl.ds(r, 1), :]
        for e in range(width + 1):
            value = lax.dot_general(
                strip[r, :, e * block :],
                strip[r + e, :, : (2 * width + 1 - e) * block],
                (((1,), (1,)), ((), ())),
                preferred_element_type=jnp.float32,
            )
            if e > 0:
                value = jnp.where(flags[:, e - 1 : e] == 1, value, 0.0)
            prod[r, e] = value.astype(prod.dtype)
        place_row = pos * block_rows + r
        pltpu.make_async_copy(prod.at[r, :, mine, :], out.at[place_row], loc_sem.at[3]).start()

        @pl.loop(0, cols_n - 1)
        def _(k):
            dst = target(k)
            pltpu.make_async_remote_copy(
                src_ref=prod.at[r, :, slab_of(dst), :],
                dst_ref=out.at[place_row],
                send_sem=out_send.at[dst],
                recv_sem=out_recv.at[col],
                device_id=(row, dst),
                device_id_type=MESH,
            ).start()

    products(0)
    arrive(2)
    place(2)

    @pl.when(pass_next)
    def _():
        for m in range(width):
            halo(1, m).wait_recv()

    @pl.when(pos == lower)
    def _():
        arrive_edge()
        place_lower()

    for d in range(1, width):

        @pl.loop(block_rows, block_rows + width - d)
        def _(r):
            strip[r + d, :, part_of(width - d)] = strip[r, :, part_of(width + d)].T

    pl.loop(1, block_rows)(products)

    @pl.when(pass_next)
    def _():
        for m in range(width):
            halo(0, m).wait_send()

    @pl.when(pass_prev)
    def _():
        for m in range(width):
            halo(1, m).wait_send()

    for way in range(2):

        @pl.when(col != edge_to[way])
        def _():
            piece = edge_piece(col)
            pltpu.make_async_copy(piece, piece, edge_send.at[way]).wait()

    def rows_of(c):
        return pl.ds(turned(c) * block_rows, block_rows)

    whole = out.at[rows_of(col)]
    pltpu.make_async_copy(whole, whole, loc_sem.at[3]).wait()

    @pl.loop(1, cols_n)
    def _(k):
        dev = other(k)
        sent = up.at[rows_of(dev)]
        pltpu.make_async_copy(sent, sent, in_send.at[dev]).wait()
        left = prod.at[:, :, slab_of(dev), :]
        pltpu.make_async_copy(left, left, out_send.at[dev]).wait()
        came = out.at[rows_of(dev)]
        pltpu.make_async_copy(came, came, out_recv.at[dev]).wait()


def shards(rows_n, cols_n, upper_tiles, occupied):
    block_rows, width = occupied.shape
    block = upper_tiles.shape[3]
    flags = jnp.pad(occupied, ((0, 0), (0, 128 - width)))
    dma = pltpu.SemaphoreType.DMA
    return pl.pallas_call(
        functools.partial(band_square_kernel, rows_n, cols_n, width),
        out_shape=jax.ShapeDtypeStruct(upper_tiles.shape, upper_tiles.dtype),
        in_specs=[pl.BlockSpec(memory_space=pl.ANY)] * 2,
        out_specs=pl.BlockSpec(memory_space=pl.ANY),
        scratch_shapes=[
            pltpu.VMEM((block_rows, width + 1, block, block), jnp.bfloat16),
            pltpu.VMEM((block_rows + width, block, (2 * width + 1) * block), jnp.bfloat16),
            pltpu.VMEM((block_rows, width + 1, block, block), jnp.bfloat16),
            pltpu.VMEM((width, width, block, block), jnp.bfloat16),
            pltpu.VMEM((block_rows, 128), jnp.int32),
            pltpu.VMEM((block_rows, 128), jnp.int32),
            pltpu.VMEM((block_rows, 128), jnp.int32),
            pltpu.VMEM((block_rows, 128), jnp.int32),
            dma((cols_n,)),
            dma((3, cols_n)),
            dma((2, width)),
            dma((2, width)),
            dma((2,)),
            dma((cols_n,)),
            dma((cols_n,)),
            dma((cols_n,)),
            dma((3,)),
            dma((4,)),
        ],
        compiler_params=pltpu.CompilerParams(
            collective_id=0, has_side_effects=True, vmem_limit_bytes=48 * 2**20
        ),
        cost_estimate=pl.CostEstimate(
            flops=2 * 35 * block_rows * block**3, bytes_accessed=2 * upper_tiles.size * 2, transcendentals=0
        ),
    )(upper_tiles, flags)


def solution(mesh):
    return jax.shard_map(
        functools.partial(shards, mesh.shape["row"], mesh.shape["col"]),
        mesh=mesh,
        in_specs=(P("row", None, "col", None), P(("row", "col"), None)),
        out_specs=P("row", None, "col", None),
        check_vma=False,
    )
```

```python
import functools

import jax
import jax.numpy as jnp
from jax import lax
from jax.experimental import pallas as pl
from jax.experimental.pallas import tpu as pltpu
from jax.sharding import PartitionSpec as P

MESH = pl.DeviceIdType.MESH


def band_square_kernel(
    rows_n,
    cols_n,
    width,
    up,
    occ,
    out,
    tiles,
    strip,
    prod,
    edge,
    occ_here,
    occ_far,
    kept,
    kept_far,
    in_send,
    in_recv,
    halo_send,
    halo_recv,
    edge_send,
    edge_recv,
    out_send,
    out_recv,
    occ_sem,
    loc_sem,
):
    block_rows, block = tiles.shape[0], tiles.shape[2]
    slab = block // cols_n
    row, col = lax.axis_index("row"), lax.axis_index("col")
    odd = lax.rem(row, 2)

    def turned(c):
        return jnp.where(odd == 1, cols_n - 1 - c, c)

    pos = turned(col)
    chunk = row * cols_n + pos
    step = 1 - 2 * odd
    lower, upper = cols_n // 2 - 1, cols_n // 2
    has_next, has_prev = chunk < rows_n * cols_n - 1, chunk > 0
    pass_next, pass_prev = has_next & (pos != lower), has_prev & (pos != upper)
    next_out, prev_out = pos == cols_n - 1, pos == 0
    next_dev = (jnp.where(next_out, row + 1, row), jnp.where(next_out, col, col + step))
    prev_dev = (jnp.where(prev_out, row - 1, row), jnp.where(prev_out, col, col - step))

    def other(k):
        return lax.rem(col + k, cols_n)

    barrier = pltpu.get_barrier_semaphore()

    @pl.loop(1, cols_n)
    def _(k):
        pl.semaphore_signal(barrier, inc=1, device_id=(row, other(k)), device_id_type=MESH)

    @pl.when(next_out & has_next)
    def _():
        pl.semaphore_signal(barrier, inc=1, device_id=next_dev, device_id_type=MESH)

    @pl.when(prev_out & has_prev)
    def _():
        pl.semaphore_signal(barrier, inc=1, device_id=prev_dev, device_id_type=MESH)

    outside = (next_out & has_next) | (prev_out & has_prev)
    pl.semaphore_wait(barrier, cols_n - 1 + jnp.where(outside, 1, 0))

    def slab_of(c):
        return pl.ds(pl.multiple_of(c * slab, slab), slab)

    def cells(stage):
        for r in range(block_rows):
            cut = width - r if r < width else block_rows - r
            first, rest = (0, cut), (cut, width + 1)
            if r >= width:
                first, rest = rest, first
            if stage == (1 if r < width else 0):
                yield r, first
            elif stage == (2 if r <= width else 3):
                yield r, rest

    def piece_of(stage, c):
        count = sum(hi - lo for _, (lo, hi) in cells(stage))
        deep = max(n for n in range(1, width + 2) if count % n == 0 and count // n <= block_rows)
        return tiles.at[: count // deep, :deep, slab_of(c), :]

    mine = slab_of(col)
    def send(stage):
        for r, (lo, hi) in cells(stage):
            pltpu.make_async_copy(
                up.at[pos * block_rows + r, lo:hi], tiles.at[r, lo:hi, mine, :], loc_sem.at[stage]
            ).start()

            @pl.loop(1, cols_n)
            def _(k):
                dst = other(k)
                pltpu.make_async_remote_copy(
                    src_ref=up.at[turned(dst) * block_rows + r, lo:hi],
                    dst_ref=tiles.at[r, lo:hi, mine, :],
                    send_sem=in_send.at[dst],
                    recv_sem=in_recv.at[stage, col],
                    device_id=(row, dst),
                    device_id_type=MESH,
                ).start()

    def edge_span(way, m):
        return (lower * block_rows + width + m, width - m, m + 1) if way == 0 else (
            upper * block_rows + m, 0, width - m)

    edge_to = (turned(upper), turned(lower))

    def send_edge(way):
        for m in range(width):
            r, lo, count = edge_span(way, m)
            src, dst = up.at[r, lo : lo + count], edge.at[m, :count, mine, :]

            @pl.when(col != edge_to[way])
            def _():
                pltpu.make_async_remote_copy(
                    src_ref=src,
                    dst_ref=dst,
                    send_sem=edge_send.at[way],
                    recv_sem=edge_recv.at[col],
                    device_id=(row, edge_to[way]),
                    device_id_type=MESH,
                ).start()

            @pl.when(col == edge_to[way])
            def _():
                pltpu.make_async_copy(src, dst, edge_recv.at[col]).start()

    def edge_piece(c):
        return tiles.at[: width // 2, : width + 1, slab_of(c), :]

    def arrive_edge():
        @pl.loop(0, cols_n)
        def _(c):
            piece = edge_piece(c)
            pltpu.make_async_copy(piece, piece, edge_recv.at[c]).wait()

    send(0)
    send_edge(0)
    send(1)
    send_edge(1)
    send(2)

    partner = cols_n - 1 - col
    occ_copy = pltpu.make_async_remote_copy(
        src_ref=occ,
        dst_ref=occ_far,
        send_sem=occ_sem.at[0],
        recv_sem=occ_sem.at[1],
        device_id=(row, partner),
        device_id_type=MESH,
    )
    occ_copy.start()
    occ_local = pltpu.make_async_copy(occ, occ_here, occ_sem.at[2])
    occ_local.start()
    occ_local.wait()
    occ_copy.wait()

    shape = kept.shape
    offset = (
        lax.broadcasted_iota(jnp.int32, shape, 0) + lax.broadcasted_iota(jnp.int32, shape, 1) + 1
    )
    total = rows_n * cols_n * block_rows
    chunk_far = row * cols_n + cols_n - 1 - pos
    flags_here, flags_far = occ_here[...], occ_far[...]
    for ref, flags, number in (
        (kept, jnp.where(odd == 1, flags_far, flags_here), chunk),
        (kept_far, jnp.where(odd == 1, flags_here, flags_far), chunk_far),
    ):
        ref[...] = jnp.where((flags == 1) & (number * block_rows + offset < total), 1, 0)

    def part_of(n):
        return slice(n * block, (n + 1) * block)

    @pl.when(jnp.logical_not(has_prev))
    def _():
        for q in range(width):
            strip[q, :, : (width - q) * block] = jnp.zeros(
                (block, (width - q) * block), strip.dtype
            )

    @pl.when(jnp.logical_not(has_next))
    def _():
        for m in range(width):
            strip[block_rows + m, :, width * block : (2 * width - m) * block] = jnp.zeros(
                (block, (width - m) * block), strip.dtype
            )

    def arrive(stage):
        piece = piece_of(stage, col)
        pltpu.make_async_copy(piece, piece, loc_sem.at[stage]).wait()

        @pl.loop(1, cols_n)
        def _(k):
            src = other(k)
            piece = piece_of(stage, src)
            pltpu.make_async_copy(piece, piece, in_recv.at[stage, src]).wait()

    def place(stage):
        for d in range(width + 1):
            lo, hi = (
                (block_rows - d, block_rows),
                (0, width - d),
                (width - d, min(width + 1, block_rows - d)),
                (width + 1, block_rows - d),
            )[stage]
            if lo >= hi:
                continue

            @pl.loop(lo, hi)
            def _(r):
                tile = tiles[r, d]
                if d == 0:
                    strip[r, :, part_of(width)] = symmetric(tile)
                else:
                    tile = masked(tile, kept[pl.ds(r, 1), :], d)
                    strip[r, :, part_of(width + d)] = tile
                    strip[r + d, :, part_of(width - d)] = tile.T

    def masked(tile, flags, d):
        return jnp.where(flags[:, d - 1 : d] == 1, tile, jnp.zeros_like(tile))

    def symmetric(tile):
        full = tile.astype(jnp.float32)
        return (0.5 * (full + full.T)).astype(strip.dtype)

    def place_upper():
        for m in range(width):
            for q in range(m + 1):
                flags = kept_far[width + m : width + m + 1, :]
                tile = masked(edge[m, q], flags, width - m + q)
                strip[q, :, part_of(m - q)] = tile.T

    def place_lower():
        for m in range(width):
            strip[block_rows + m, :, part_of(width)] = symmetric(edge[m, 0])
            for d in range(1, width - m):
                flags = kept_far[m : m + 1, :]
                strip[block_rows + m, :, part_of(width + d)] = masked(edge[m, d], flags, d)

    def halo(way, m):
        if way == 0:
            cut = slice(0, (width - m) * block)
            src, dst, dev = block_rows + m, m, next_dev
        else:
            cut = slice(width * block, (2 * width - m) * block)
            src, dst, dev = m, block_rows + m, prev_dev
        return pltpu.make_async_remote_copy(
            src_ref=strip.at[src, :, cut],
            dst_ref=strip.at[dst, :, cut],
            send_sem=halo_send.at[way, m],
            recv_sem=halo_recv.at[way, m],
            device_id=dev,
            device_id_type=MESH,
        )

    arrive(0)
    place(0)

    @pl.when(pass_next)
    def _():
        for m in range(width):
            halo(0, m).start()

    arrive(1)
    send(3)
    place(1)

    @pl.when(pass_prev)
    def _():
        for m in range(width):
            halo(1, m).start()

    arrive(2)
    place(2)

    @pl.when(pass_prev)
    def _():
        for m in range(width):
            halo(0, m).wait_recv()

    @pl.when(pos == upper)
    def _():
        arrive_edge()
        place_upper()

    def products(r):
        flags = kept[pl.ds(r, 1), :]
        for e in range(width + 1):
            value = lax.dot_general(
                strip[r, :, e * block :],
                strip[r + e, :, : (2 * width + 1 - e) * block],
                (((1,), (1,)), ((), ())),
                preferred_element_type=jnp.float32,
            )
            if e > 0:
                value = jnp.where(flags[:, e - 1 : e] == 1, value, 0.0)
            prod[r, e] = value.astype(prod.dtype)
        place_row = pos * block_rows + r
        pltpu.make_async_copy(prod.at[r, :, mine, :], out.at[place_row], loc_sem.at[4]).start()

        @pl.loop(1, cols_n)
        def _(k):
            dst = other(k)
            pltpu.make_async_remote_copy(
                src_ref=prod.at[r, :, slab_of(dst), :],
                dst_ref=out.at[place_row],
                send_sem=out_send.at[dst],
                recv_sem=out_recv.at[col],
                device_id=(row, dst),
                device_id_type=MESH,
            ).start()

    products(0)
    arrive(3)
    place(3)

    @pl.when(pass_next)
    def _():
        for m in range(width):
            halo(1, m).wait_recv()

    @pl.when(pos == lower)
    def _():
        arrive_edge()
        place_lower()

    for d in range(1, width):

        @pl.loop(block_rows, block_rows + width - d)
        def _(r):
            strip[r + d, :, part_of(width - d)] = strip[r, :, part_of(width + d)].T

    pl.loop(1, block_rows)(products)

    @pl.when(pass_next)
    def _():
        for m in range(width):
            halo(0, m).wait_send()

    @pl.when(pass_prev)
    def _():
        for m in range(width):
            halo(1, m).wait_send()

    for way in range(2):

        @pl.when(col != edge_to[way])
        def _():
            piece = edge_piece(col)
            pltpu.make_async_copy(piece, piece, edge_send.at[way]).wait()

    def rows_of(c):
        return pl.ds(turned(c) * block_rows, block_rows)

    whole = out.at[rows_of(col)]
    pltpu.make_async_copy(whole, whole, loc_sem.at[4]).wait()

    @pl.loop(1, cols_n)
    def _(k):
        dev = other(k)
        sent = up.at[rows_of(dev)]
        pltpu.make_async_copy(sent, sent, in_send.at[dev]).wait()
        left = prod.at[:, :, slab_of(dev), :]
        pltpu.make_async_copy(left, left, out_send.at[dev]).wait()
        came = out.at[rows_of(dev)]
        pltpu.make_async_copy(came, came, out_recv.at[dev]).wait()


def shards(rows_n, cols_n, upper_tiles, occupied):
    block_rows, width = occupied.shape
    block = upper_tiles.shape[3]
    flags = jnp.pad(occupied, ((0, 0), (0, 128 - width)))
    dma = pltpu.SemaphoreType.DMA
    return pl.pallas_call(
        functools.partial(band_square_kernel, rows_n, cols_n, width),
        out_shape=jax.ShapeDtypeStruct(upper_tiles.shape, upper_tiles.dtype),
        in_specs=[pl.BlockSpec(memory_space=pl.ANY)] * 2,
        out_specs=pl.BlockSpec(memory_space=pl.ANY),
        scratch_shapes=[
            pltpu.VMEM((block_rows, width + 1, block, block), jnp.bfloat16),
            pltpu.VMEM((block_rows + width, block, (2 * width + 1) * block), jnp.bfloat16),
            pltpu.VMEM((block_rows, width + 1, block, block), jnp.bfloat16),
            pltpu.VMEM((width, width, block, block), jnp.bfloat16),
            pltpu.VMEM((block_rows, 128), jnp.int32),
            pltpu.VMEM((block_rows, 128), jnp.int32),
            pltpu.VMEM((block_rows, 128), jnp.int32),
            pltpu.VMEM((block_rows, 128), jnp.int32),
            dma((cols_n,)),
            dma((4, cols_n)),
            dma((2, width)),
            dma((2, width)),
            dma((2,)),
            dma((cols_n,)),
            dma((cols_n,)),
            dma((cols_n,)),
            dma((3,)),
            dma((5,)),
        ],
        compiler_params=pltpu.CompilerParams(
            collective_id=0, has_side_effects=True, vmem_limit_bytes=48 * 2**20
        ),
        cost_estimate=pl.CostEstimate(
            flops=2 * 35 * block_rows * block**3, bytes_accessed=2 * upper_tiles.size * 2, transcendentals=0
        ),
    )(upper_tiles, flags)


def solution(mesh):
    return jax.shard_map(
        functools.partial(shards, mesh.shape["row"], mesh.shape["col"]),
        mesh=mesh,
        in_specs=(P("row", None, "col", None), P(("row", "col"), None)),
        out_specs=P("row", None, "col", None),
        check_vma=False,
    )
```

```python
import functools

import jax
import jax.numpy as jnp
from jax import lax
from jax.experimental import pallas as pl
from jax.experimental.pallas import tpu as pltpu
from jax.sharding import PartitionSpec as P

MESH = pl.DeviceIdType.MESH


def band_square_kernel(
    rows_n,
    cols_n,
    width,
    up,
    occ,
    out,
    tiles,
    strip,
    prod,
    edge,
    occ_here,
    occ_far,
    kept,
    kept_far,
    in_send,
    in_recv,
    halo_send,
    halo_recv,
    edge_send,
    edge_recv,
    out_send,
    out_recv,
    occ_sem,
    loc_sem,
):
    block_rows, block = tiles.shape[0], tiles.shape[2]
    slab = block // cols_n
    row, col = lax.axis_index("row"), lax.axis_index("col")
    odd = lax.rem(row, 2)

    def turned(c):
        return jnp.where(odd == 1, cols_n - 1 - c, c)

    pos = turned(col)
    chunk = row * cols_n + pos
    step = 1 - 2 * odd
    lower, upper = cols_n // 2 - 1, cols_n // 2
    has_next, has_prev = chunk < rows_n * cols_n - 1, chunk > 0
    pass_next, pass_prev = has_next & (pos != lower), has_prev & (pos != upper)
    next_out, prev_out = pos == cols_n - 1, pos == 0
    next_dev = (jnp.where(next_out, row + 1, row), jnp.where(next_out, col, col + step))
    prev_dev = (jnp.where(prev_out, row - 1, row), jnp.where(prev_out, col, col - step))

    def other(k):
        return lax.rem(col + k, cols_n)

    barrier = pltpu.get_barrier_semaphore()

    @pl.loop(1, cols_n)
    def _(k):
        pl.semaphore_signal(barrier, inc=1, device_id=(row, other(k)), device_id_type=MESH)

    @pl.when(next_out & has_next)
    def _():
        pl.semaphore_signal(barrier, inc=1, device_id=next_dev, device_id_type=MESH)

    @pl.when(prev_out & has_prev)
    def _():
        pl.semaphore_signal(barrier, inc=1, device_id=prev_dev, device_id_type=MESH)

    outside = (next_out & has_next) | (prev_out & has_prev)
    pl.semaphore_wait(barrier, cols_n - 1 + jnp.where(outside, 1, 0))

    def slab_of(c):
        return pl.ds(pl.multiple_of(c * slab, slab), slab)

    def cells(stage):
        for r in range(block_rows):
            cut = width - r if r < width else block_rows - r
            first, rest = (0, cut), (cut, width + 1)
            if r >= width:
                first, rest = rest, first
            if stage == (1 if r < width else 0):
                yield r, first
            elif stage == (2 if r <= width else 3):
                yield r, rest

    def piece_of(stage, c):
        count = sum(hi - lo for _, (lo, hi) in cells(stage))
        deep = max(n for n in range(1, width + 2) if count % n == 0 and count // n <= block_rows)
        return tiles.at[: count // deep, :deep, slab_of(c), :]

    mine = slab_of(col)
    chunks = [(stage, r, lo, hi) for stage in range(4) for r, (lo, hi) in cells(stage)]
    ahead = 3

    def chunk_copy(n, dst):
        stage, r, lo, hi = chunks[n]
        return pltpu.make_async_remote_copy(
            src_ref=up.at[turned(dst) * block_rows + r, lo:hi],
            dst_ref=tiles.at[r, lo:hi, mine, :],
            send_sem=in_send.at[n % ahead, dst],
            recv_sem=in_recv.at[stage, col],
            device_id=(row, dst),
            device_id_type=MESH,
        )

    def send(first, last):
        for n in range(first, last):
            stage, r, lo, hi = chunks[n]
            pltpu.make_async_copy(
                up.at[pos * block_rows + r, lo:hi], tiles.at[r, lo:hi, mine, :], loc_sem.at[stage]
            ).start()

            @pl.loop(1, cols_n)
            def _(k):
                dst = other(k)
                if n >= ahead:
                    chunk_copy(n - ahead, dst).wait_send()
                chunk_copy(n, dst).start()

    starts = [min(n for n, chunk in enumerate(chunks) if chunk[0] == stage) for stage in range(4)]

    def edge_span(way, m):
        return (lower * block_rows + width + m, width - m, m + 1) if way == 0 else (
            upper * block_rows + m, 0, width - m)

    edge_to = (turned(upper), turned(lower))

    def send_edge(way):
        for m in range(width):
            r, lo, count = edge_span(way, m)
            src, dst = up.at[r, lo : lo + count], edge.at[m, :count, mine, :]

            @pl.when(col != edge_to[way])
            def _():
                pltpu.make_async_remote_copy(
                    src_ref=src,
                    dst_ref=dst,
                    send_sem=edge_send.at[way],
                    recv_sem=edge_recv.at[col],
                    device_id=(row, edge_to[way]),
                    device_id_type=MESH,
                ).start()

            @pl.when(col == edge_to[way])
            def _():
                pltpu.make_async_copy(src, dst, edge_recv.at[col]).start()

    def edge_piece(c):
        return tiles.at[: width // 2, : width + 1, slab_of(c), :]

    def arrive_edge():
        @pl.loop(0, cols_n)
        def _(c):
            piece = edge_piece(c)
            pltpu.make_async_copy(piece, piece, edge_recv.at[c]).wait()

    send(starts[0], starts[1])
    send_edge(0)
    send(starts[1], starts[2])
    send_edge(1)

    partner = cols_n - 1 - col
    occ_copy = pltpu.make_async_remote_copy(
        src_ref=occ,
        dst_ref=occ_far,
        send_sem=occ_sem.at[0],
        recv_sem=occ_sem.at[1],
        device_id=(row, partner),
        device_id_type=MESH,
    )
    occ_copy.start()
    occ_local = pltpu.make_async_copy(occ, occ_here, occ_sem.at[2])
    occ_local.start()
    occ_local.wait()
    occ_copy.wait()

    shape = kept.shape
    offset = (
        lax.broadcasted_iota(jnp.int32, shape, 0) + lax.broadcasted_iota(jnp.int32, shape, 1) + 1
    )
    total = rows_n * cols_n * block_rows
    chunk_far = row * cols_n + cols_n - 1 - pos
    flags_here, flags_far = occ_here[...], occ_far[...]
    for ref, flags, number in (
        (kept, jnp.where(odd == 1, flags_far, flags_here), chunk),
        (kept_far, jnp.where(odd == 1, flags_here, flags_far), chunk_far),
    ):
        ref[...] = jnp.where((flags == 1) & (number * block_rows + offset < total), 1, 0)

    def part_of(n):
        return slice(n * block, (n + 1) * block)

    @pl.when(jnp.logical_not(has_prev))
    def _():
        for q in range(width):
            strip[q, :, : (width - q) * block] = jnp.zeros(
                (block, (width - q) * block), strip.dtype
            )

    @pl.when(jnp.logical_not(has_next))
    def _():
        for m in range(width):
            strip[block_rows + m, :, width * block : (2 * width - m) * block] = jnp.zeros(
                (block, (width - m) * block), strip.dtype
            )

    def arrive(stage):
        piece = piece_of(stage, col)
        pltpu.make_async_copy(piece, piece, loc_sem.at[stage]).wait()

        @pl.loop(1, cols_n)
        def _(k):
            src = other(k)
            piece = piece_of(stage, src)
            pltpu.make_async_copy(piece, piece, in_recv.at[stage, src]).wait()

    def place(stage):
        for d in range(width + 1):
            lo, hi = (
                (block_rows - d, block_rows),
                (0, width - d),
                (width - d, min(width + 1, block_rows - d)),
                (width + 1, block_rows - d),
            )[stage]
            if lo >= hi:
                continue

            @pl.loop(lo, hi)
            def _(r):
                tile = tiles[r, d]
                if d == 0:
                    strip[r, :, part_of(width)] = symmetric(tile)
                else:
                    tile = masked(tile, kept[pl.ds(r, 1), :], d)
                    strip[r, :, part_of(width + d)] = tile
                    strip[r + d, :, part_of(width - d)] = tile.T

    def masked(tile, flags, d):
        return jnp.where(flags[:, d - 1 : d] == 1, tile, jnp.zeros_like(tile))

    def symmetric(tile):
        full = tile.astype(jnp.float32)
        return (0.5 * (full + full.T)).astype(strip.dtype)

    def place_upper():
        for m in range(width):
            for q in range(m + 1):
                flags = kept_far[width + m : width + m + 1, :]
                tile = masked(edge[m, q], flags, width - m + q)
                strip[q, :, part_of(m - q)] = tile.T

    def place_lower():
        for m in range(width):
            strip[block_rows + m, :, part_of(width)] = symmetric(edge[m, 0])
            for d in range(1, width - m):
                flags = kept_far[m : m + 1, :]
                strip[block_rows + m, :, part_of(width + d)] = masked(edge[m, d], flags, d)

    def halo(way, m):
        if way == 0:
            cut = slice(0, (width - m) * block)
            src, dst, dev = block_rows + m, m, next_dev
        else:
            cut = slice(width * block, (2 * width - m) * block)
            src, dst, dev = m, block_rows + m, prev_dev
        return pltpu.make_async_remote_copy(
            src_ref=strip.at[src, :, cut],
            dst_ref=strip.at[dst, :, cut],
            send_sem=halo_send.at[way, m],
            recv_sem=halo_recv.at[way, m],
            device_id=dev,
            device_id_type=MESH,
        )

    arrive(0)
    place(0)

    @pl.when(pass_next)
    def _():
        for m in range(width):
            halo(0, m).start()

    send(starts[2], starts[2] + ahead)
    arrive(1)
    place(1)

    @pl.when(pass_prev)
    def _():
        for m in range(width):
            halo(1, m).start()

    send(starts[2] + ahead, len(chunks))
    arrive(2)
    place(2)

    @pl.when(pass_prev)
    def _():
        for m in range(width):
            halo(0, m).wait_recv()

    @pl.when(pos == upper)
    def _():
        arrive_edge()
        place_upper()

    def products(r):
        flags = kept[pl.ds(r, 1), :]
        for e in range(width + 1):
            value = lax.dot_general(
                strip[r, :, e * block :],
                strip[r + e, :, : (2 * width + 1 - e) * block],
                (((1,), (1,)), ((), ())),
                preferred_element_type=jnp.float32,
            )
            if e > 0:
                value = jnp.where(flags[:, e - 1 : e] == 1, value, 0.0)
            prod[r, e] = value.astype(prod.dtype)
        place_row = pos * block_rows + r
        pltpu.make_async_copy(prod.at[r, :, mine, :], out.at[place_row], loc_sem.at[4]).start()

        @pl.loop(1, cols_n)
        def _(k):
            dst = other(k)
            pltpu.make_async_remote_copy(
                src_ref=prod.at[r, :, slab_of(dst), :],
                dst_ref=out.at[place_row],
                send_sem=out_send.at[dst],
                recv_sem=out_recv.at[col],
                device_id=(row, dst),
                device_id_type=MESH,
            ).start()

    products(0)
    arrive(3)
    place(3)

    @pl.when(pass_next)
    def _():
        for m in range(width):
            halo(1, m).wait_recv()

    @pl.when(pos == lower)
    def _():
        arrive_edge()
        place_lower()

    for d in range(1, width):

        @pl.loop(block_rows, block_rows + width - d)
        def _(r):
            strip[r + d, :, part_of(width - d)] = strip[r, :, part_of(width + d)].T

    pl.loop(1, block_rows)(products)

    @pl.when(pass_next)
    def _():
        for m in range(width):
            halo(0, m).wait_send()

    @pl.when(pass_prev)
    def _():
        for m in range(width):
            halo(1, m).wait_send()

    for way in range(2):

        @pl.when(col != edge_to[way])
        def _():
            piece = edge_piece(col)
            pltpu.make_async_copy(piece, piece, edge_send.at[way]).wait()

    def rows_of(c):
        return pl.ds(turned(c) * block_rows, block_rows)

    whole = out.at[rows_of(col)]
    pltpu.make_async_copy(whole, whole, loc_sem.at[4]).wait()

    @pl.loop(1, cols_n)
    def _(k):
        dev = other(k)
        for n in range(len(chunks) - ahead, len(chunks)):
            chunk_copy(n, dev).wait_send()
        left = prod.at[:, :, slab_of(dev), :]
        pltpu.make_async_copy(left, left, out_send.at[dev]).wait()
        came = out.at[rows_of(dev)]
        pltpu.make_async_copy(came, came, out_recv.at[dev]).wait()


def shards(rows_n, cols_n, upper_tiles, occupied):
    block_rows, width = occupied.shape
    block = upper_tiles.shape[3]
    flags = jnp.pad(occupied, ((0, 0), (0, 128 - width)))
    dma = pltpu.SemaphoreType.DMA
    return pl.pallas_call(
        functools.partial(band_square_kernel, rows_n, cols_n, width),
        out_shape=jax.ShapeDtypeStruct(upper_tiles.shape, upper_tiles.dtype),
        in_specs=[pl.BlockSpec(memory_space=pl.ANY)] * 2,
        out_specs=pl.BlockSpec(memory_space=pl.ANY),
        scratch_shapes=[
            pltpu.VMEM((block_rows, width + 1, block, block), jnp.bfloat16),
            pltpu.VMEM((block_rows + width, block, (2 * width + 1) * block), jnp.bfloat16),
            pltpu.VMEM((block_rows, width + 1, block, block), jnp.bfloat16),
            pltpu.VMEM((width, width, block, block), jnp.bfloat16),
            pltpu.VMEM((block_rows, 128), jnp.int32),
            pltpu.VMEM((block_rows, 128), jnp.int32),
            pltpu.VMEM((block_rows, 128), jnp.int32),
            pltpu.VMEM((block_rows, 128), jnp.int32),
            dma((3, cols_n)),
            dma((4, cols_n)),
            dma((2, width)),
            dma((2, width)),
            dma((2,)),
            dma((cols_n,)),
            dma((cols_n,)),
            dma((cols_n,)),
            dma((3,)),
            dma((5,)),
        ],
        compiler_params=pltpu.CompilerParams(
            collective_id=0, has_side_effects=True, vmem_limit_bytes=48 * 2**20
        ),
        cost_estimate=pl.CostEstimate(
            flops=2 * 35 * block_rows * block**3, bytes_accessed=2 * upper_tiles.size * 2, transcendentals=0
        ),
    )(upper_tiles, flags)


def solution(mesh):
    return jax.shard_map(
        functools.partial(shards, mesh.shape["row"], mesh.shape["col"]),
        mesh=mesh,
        in_specs=(P("row", None, "col", None), P(("row", "col"), None)),
        out_specs=P("row", None, "col", None),
        check_vma=False,
    )
```

```python
import functools

import jax
import jax.numpy as jnp
from jax import lax
from jax.experimental import pallas as pl
from jax.experimental.pallas import tpu as pltpu
from jax.sharding import PartitionSpec as P

MESH = pl.DeviceIdType.MESH


def band_square_kernel(
    rows_n,
    cols_n,
    width,
    up,
    occ,
    out,
    tiles,
    strip,
    prod,
    edge,
    occ_here,
    occ_far,
    kept,
    kept_far,
    in_send,
    in_recv,
    halo_send,
    halo_recv,
    edge_send,
    edge_recv,
    out_send,
    out_recv,
    occ_sem,
    loc_sem,
):
    block_rows, block = tiles.shape[0], tiles.shape[2]
    slab = block // cols_n
    row, col = lax.axis_index("row"), lax.axis_index("col")
    odd = lax.rem(row, 2)

    def turned(c):
        return jnp.where(odd == 1, cols_n - 1 - c, c)

    pos = turned(col)
    chunk = row * cols_n + pos
    step = 1 - 2 * odd
    lower, upper = cols_n // 2 - 1, cols_n // 2
    has_next, has_prev = chunk < rows_n * cols_n - 1, chunk > 0
    pass_next, pass_prev = has_next & (pos != lower), has_prev & (pos != upper)
    next_out, prev_out = pos == cols_n - 1, pos == 0
    next_dev = (jnp.where(next_out, row + 1, row), jnp.where(next_out, col, col + step))
    prev_dev = (jnp.where(prev_out, row - 1, row), jnp.where(prev_out, col, col - step))

    def other(k):
        return lax.rem(col + k, cols_n)

    barrier = pltpu.get_barrier_semaphore()

    @pl.loop(1, cols_n)
    def _(k):
        pl.semaphore_signal(barrier, inc=1, device_id=(row, other(k)), device_id_type=MESH)

    @pl.when(next_out & has_next)
    def _():
        pl.semaphore_signal(barrier, inc=1, device_id=next_dev, device_id_type=MESH)

    @pl.when(prev_out & has_prev)
    def _():
        pl.semaphore_signal(barrier, inc=1, device_id=prev_dev, device_id_type=MESH)

    outside = (next_out & has_next) | (prev_out & has_prev)
    pl.semaphore_wait(barrier, cols_n - 1 + jnp.where(outside, 1, 0))

    def slab_of(c):
        return pl.ds(pl.multiple_of(c * slab, slab), slab)

    def cells(stage):
        for r in range(block_rows):
            cut = width - r if r < width else block_rows - r
            first, rest = (0, cut), (cut, width + 1)
            if r >= width:
                first, rest = rest, first
            if stage == 0:
                yield r, first
            elif (stage == 1) == (r <= width):
                yield r, rest

    def piece_of(stage, c):
        count = sum(hi - lo for _, (lo, hi) in cells(stage))
        deep = max(n for n in range(1, width + 2) if count % n == 0 and count // n <= block_rows)
        return tiles.at[: count // deep, :deep, slab_of(c), :]

    mine = slab_of(col)
    def send(stage):
        for r, (lo, hi) in cells(stage):
            pltpu.make_async_copy(
                up.at[pos * block_rows + r, lo:hi], tiles.at[r, lo:hi, mine, :], loc_sem.at[stage]
            ).start()

            @pl.loop(1, cols_n)
            def _(k):
                dst = other(k)
                pltpu.make_async_remote_copy(
                    src_ref=up.at[turned(dst) * block_rows + r, lo:hi],
                    dst_ref=tiles.at[r, lo:hi, mine, :],
                    send_sem=in_send.at[dst],
                    recv_sem=in_recv.at[stage, col],
                    device_id=(row, dst),
                    device_id_type=MESH,
                ).start()

    def edge_span(way, m):
        return (lower * block_rows + width + m, width - m, m + 1) if way == 0 else (
            upper * block_rows + m, 0, width - m)

    edge_to = (turned(upper), turned(lower))

    def send_edge(way):
        for m in range(width):
            r, lo, count = edge_span(way, m)
            src, dst = up.at[r, lo : lo + count], edge.at[m, :count, mine, :]

            @pl.when(col != edge_to[way])
            def _():
                pltpu.make_async_remote_copy(
                    src_ref=src,
                    dst_ref=dst,
                    send_sem=edge_send.at[way],
                    recv_sem=edge_recv.at[col],
                    device_id=(row, edge_to[way]),
                    device_id_type=MESH,
                ).start()

            @pl.when(col == edge_to[way])
            def _():
                pltpu.make_async_copy(src, dst, edge_recv.at[col]).start()

    def edge_piece(c):
        return tiles.at[: width // 2, : width + 1, slab_of(c), :]

    def arrive_edge():
        @pl.loop(0, cols_n)
        def _(c):
            piece = edge_piece(c)
            pltpu.make_async_copy(piece, piece, edge_recv.at[c]).wait()

    send(0)
    send_edge(0)
    send_edge(1)
    send(1)

    partner = cols_n - 1 - col
    occ_copy = pltpu.make_async_remote_copy(
        src_ref=occ,
        dst_ref=occ_far,
        send_sem=occ_sem.at[0],
        recv_sem=occ_sem.at[1],
        device_id=(row, partner),
        device_id_type=MESH,
    )
    occ_copy.start()
    occ_local = pltpu.make_async_copy(occ, occ_here, occ_sem.at[2])
    occ_local.start()
    occ_local.wait()
    occ_copy.wait()

    shape = kept.shape
    offset = (
        lax.broadcasted_iota(jnp.int32, shape, 0) + lax.broadcasted_iota(jnp.int32, shape, 1) + 1
    )
    total = rows_n * cols_n * block_rows
    chunk_far = row * cols_n + cols_n - 1 - pos
    flags_here, flags_far = occ_here[...], occ_far[...]
    for ref, flags, number in (
        (kept, jnp.where(odd == 1, flags_far, flags_here), chunk),
        (kept_far, jnp.where(odd == 1, flags_here, flags_far), chunk_far),
    ):
        ref[...] = jnp.where((flags == 1) & (number * block_rows + offset < total), 1, 0)

    def part_of(n):
        return slice(n * block, (n + 1) * block)

    @pl.when(jnp.logical_not(has_prev))
    def _():
        for q in range(width):
            strip[q, :, : (width - q) * block] = jnp.zeros(
                (block, (width - q) * block), strip.dtype
            )

    @pl.when(jnp.logical_not(has_next))
    def _():
        for m in range(width):
            strip[block_rows + m, :, width * block : (2 * width - m) * block] = jnp.zeros(
                (block, (width - m) * block), strip.dtype
            )

    def arrive(stage):
        piece = piece_of(stage, col)
        pltpu.make_async_copy(piece, piece, loc_sem.at[stage]).wait()

        @pl.loop(1, cols_n)
        def _(k):
            src = other(k)
            piece = piece_of(stage, src)
            pltpu.make_async_copy(piece, piece, in_recv.at[stage, src]).wait()

    def place(part):
        for d in range(width + 1):
            lo, hi = (
                (block_rows - d, block_rows),
                (0, width - d),
                (width - d, min(width + 1, block_rows - d)),
                (width + 1, block_rows - d),
            )[part]
            if lo >= hi:
                continue

            @pl.loop(lo, hi)
            def _(r):
                tile = tiles[r, d]
                if d == 0:
                    strip[r, :, part_of(width)] = symmetric(tile)
                else:
                    tile = masked(tile, kept[pl.ds(r, 1), :], d)
                    strip[r, :, part_of(width + d)] = tile
                    strip[r + d, :, part_of(width - d)] = tile.T

    def masked(tile, flags, d):
        return jnp.where(flags[:, d - 1 : d] == 1, tile, jnp.zeros_like(tile))

    def symmetric(tile):
        full = tile.astype(jnp.float32)
        return (0.5 * (full + full.T)).astype(strip.dtype)

    def place_upper():
        for m in range(width):
            for q in range(m + 1):
                flags = kept_far[width + m : width + m + 1, :]
                tile = masked(edge[m, q], flags, width - m + q)
                strip[q, :, part_of(m - q)] = tile.T

    def place_lower():
        for m in range(width):
            strip[block_rows + m, :, part_of(width)] = symmetric(edge[m, 0])
            for d in range(1, width - m):
                flags = kept_far[m : m + 1, :]
                strip[block_rows + m, :, part_of(width + d)] = masked(edge[m, d], flags, d)

    def halo(way, m):
        if way == 0:
            cut = slice(0, (width - m) * block)
            src, dst, dev = block_rows + m, m, next_dev
        else:
            cut = slice(width * block, (2 * width - m) * block)
            src, dst, dev = m, block_rows + m, prev_dev
        return pltpu.make_async_remote_copy(
            src_ref=strip.at[src, :, cut],
            dst_ref=strip.at[dst, :, cut],
            send_sem=halo_send.at[way, m],
            recv_sem=halo_recv.at[way, m],
            device_id=dev,
            device_id_type=MESH,
        )

    arrive(0)
    send(2)
    place(0)

    @pl.when(pass_next)
    def _():
        for m in range(width):
            halo(0, m).start()

    place(1)

    @pl.when(pass_prev)
    def _():
        for m in range(width):
            halo(1, m).start()

    arrive(1)
    place(2)

    @pl.when(pass_prev)
    def _():
        for m in range(width):
            halo(0, m).wait_recv()

    @pl.when(pos == upper)
    def _():
        arrive_edge()
        place_upper()

    def products(r):
        flags = kept[pl.ds(r, 1), :]
        for e in range(width + 1):
            value = lax.dot_general(
                strip[r, :, e * block :],
                strip[r + e, :, : (2 * width + 1 - e) * block],
                (((1,), (1,)), ((), ())),
                preferred_element_type=jnp.float32,
            )
            if e > 0:
                value = jnp.where(flags[:, e - 1 : e] == 1, value, 0.0)
            prod[r, e] = value.astype(prod.dtype)
        place_row = pos * block_rows + r
        pltpu.make_async_copy(prod.at[r, :, mine, :], out.at[place_row], loc_sem.at[3]).start()

        @pl.loop(1, cols_n)
        def _(k):
            dst = other(k)
            pltpu.make_async_remote_copy(
                src_ref=prod.at[r, :, slab_of(dst), :],
                dst_ref=out.at[place_row],
                send_sem=out_send.at[dst],
                recv_sem=out_recv.at[col],
                device_id=(row, dst),
                device_id_type=MESH,
            ).start()

    products(0)
    arrive(2)
    place(3)

    @pl.when(pass_next)
    def _():
        for m in range(width):
            halo(1, m).wait_recv()

    @pl.when(pos == lower)
    def _():
        arrive_edge()
        place_lower()

    for d in range(1, width):

        @pl.loop(block_rows, block_rows + width - d)
        def _(r):
            strip[r + d, :, part_of(width - d)] = strip[r, :, part_of(width + d)].T

    pl.loop(1, block_rows)(products)

    @pl.when(pass_next)
    def _():
        for m in range(width):
            halo(0, m).wait_send()

    @pl.when(pass_prev)
    def _():
        for m in range(width):
            halo(1, m).wait_send()

    for way in range(2):

        @pl.when(col != edge_to[way])
        def _():
            piece = edge_piece(col)
            pltpu.make_async_copy(piece, piece, edge_send.at[way]).wait()

    def rows_of(c):
        return pl.ds(turned(c) * block_rows, block_rows)

    whole = out.at[rows_of(col)]
    pltpu.make_async_copy(whole, whole, loc_sem.at[3]).wait()

    @pl.loop(1, cols_n)
    def _(k):
        dev = other(k)
        sent = up.at[rows_of(dev)]
        pltpu.make_async_copy(sent, sent, in_send.at[dev]).wait()
        left = prod.at[:, :, slab_of(dev), :]
        pltpu.make_async_copy(left, left, out_send.at[dev]).wait()
        came = out.at[rows_of(dev)]
        pltpu.make_async_copy(came, came, out_recv.at[dev]).wait()


def shards(rows_n, cols_n, upper_tiles, occupied):
    block_rows, width = occupied.shape
    block = upper_tiles.shape[3]
    flags = jnp.pad(occupied, ((0, 0), (0, 128 - width)))
    dma = pltpu.SemaphoreType.DMA
    return pl.pallas_call(
        functools.partial(band_square_kernel, rows_n, cols_n, width),
        out_shape=jax.ShapeDtypeStruct(upper_tiles.shape, upper_tiles.dtype),
        in_specs=[pl.BlockSpec(memory_space=pl.ANY)] * 2,
        out_specs=pl.BlockSpec(memory_space=pl.ANY),
        scratch_shapes=[
            pltpu.VMEM((block_rows, width + 1, block, block), jnp.bfloat16),
            pltpu.VMEM((block_rows + width, block, (2 * width + 1) * block), jnp.bfloat16),
            pltpu.VMEM((block_rows, width + 1, block, block), jnp.bfloat16),
            pltpu.VMEM((width, width, block, block), jnp.bfloat16),
            pltpu.VMEM((block_rows, 128), jnp.int32),
            pltpu.VMEM((block_rows, 128), jnp.int32),
            pltpu.VMEM((block_rows, 128), jnp.int32),
            pltpu.VMEM((block_rows, 128), jnp.int32),
            dma((cols_n,)),
            dma((3, cols_n)),
            dma((2, width)),
            dma((2, width)),
            dma((2,)),
            dma((cols_n,)),
            dma((cols_n,)),
            dma((cols_n,)),
            dma((3,)),
            dma((4,)),
        ],
        compiler_params=pltpu.CompilerParams(
            collective_id=0, has_side_effects=True, vmem_limit_bytes=48 * 2**20
        ),
        cost_estimate=pl.CostEstimate(
            flops=2 * 35 * block_rows * block**3, bytes_accessed=2 * upper_tiles.size * 2, transcendentals=0
        ),
    )(upper_tiles, flags)


def solution(mesh):
    return jax.shard_map(
        functools.partial(shards, mesh.shape["row"], mesh.shape["col"]),
        mesh=mesh,
        in_specs=(P("row", None, "col", None), P(("row", "col"), None)),
        out_specs=P("row", None, "col", None),
        check_vma=False,
    )
```

```python
import functools

import jax
import jax.numpy as jnp
from jax import lax
from jax.experimental import pallas as pl
from jax.experimental.pallas import tpu as pltpu
from jax.sharding import PartitionSpec as P

MESH = pl.DeviceIdType.MESH


def band_square_kernel(
    rows_n,
    cols_n,
    width,
    up,
    occ,
    out,
    tiles,
    strip,
    prod,
    edge,
    occ_here,
    occ_far,
    kept,
    kept_far,
    in_send,
    in_recv,
    halo_send,
    halo_recv,
    edge_send,
    edge_recv,
    out_send,
    out_recv,
    occ_sem,
    loc_sem,
):
    block_rows, block = tiles.shape[0], tiles.shape[2]
    slab = block // cols_n
    row, col = lax.axis_index("row"), lax.axis_index("col")
    odd = lax.rem(row, 2)

    def turned(c):
        return jnp.where(odd == 1, cols_n - 1 - c, c)

    pos = turned(col)
    chunk = row * cols_n + pos
    step = 1 - 2 * odd
    lower, upper = cols_n // 2 - 1, cols_n // 2
    has_next, has_prev = chunk < rows_n * cols_n - 1, chunk > 0
    pass_next, pass_prev = has_next & (pos != lower), has_prev & (pos != upper)
    next_out, prev_out = pos == cols_n - 1, pos == 0
    next_dev = (jnp.where(next_out, row + 1, row), jnp.where(next_out, col, col + step))
    prev_dev = (jnp.where(prev_out, row - 1, row), jnp.where(prev_out, col, col - step))

    def other(k):
        return lax.rem(col + k, cols_n)

    barrier = pltpu.get_barrier_semaphore()

    @pl.loop(1, cols_n)
    def _(k):
        pl.semaphore_signal(barrier, inc=1, device_id=(row, other(k)), device_id_type=MESH)

    @pl.when(next_out & has_next)
    def _():
        pl.semaphore_signal(barrier, inc=1, device_id=next_dev, device_id_type=MESH)

    @pl.when(prev_out & has_prev)
    def _():
        pl.semaphore_signal(barrier, inc=1, device_id=prev_dev, device_id_type=MESH)

    outside = (next_out & has_next) | (prev_out & has_prev)
    pl.semaphore_wait(barrier, cols_n - 1 + jnp.where(outside, 1, 0))

    def slab_of(c):
        return pl.ds(pl.multiple_of(c * slab, slab), slab)

    def cells(stage):
        for r in range(block_rows):
            cut = width - r if r < width else block_rows - r
            first, rest = (0, cut), (cut, width + 1)
            if r >= width:
                first, rest = rest, first
            if stage == 0:
                yield r, first
            elif (stage == 1) == (r <= width):
                yield r, rest

    def piece_of(stage, c):
        count = sum(hi - lo for _, (lo, hi) in cells(stage))
        deep = max(n for n in range(1, width + 2) if count % n == 0 and count // n <= block_rows)
        return tiles.at[: count // deep, :deep, slab_of(c), :]

    mine = slab_of(col)
    def send_cell(stage, cell, dst):
        r, (lo, hi) = cell
        pltpu.make_async_remote_copy(
            src_ref=up.at[turned(dst) * block_rows + r, lo:hi],
            dst_ref=tiles.at[r, lo:hi, mine, :],
            send_sem=in_send.at[dst],
            recv_sem=in_recv.at[stage, col],
            device_id=(row, dst),
            device_id_type=MESH,
        ).start()

    def keep_own(stage):
        for r, (lo, hi) in cells(stage):
            pltpu.make_async_copy(
                up.at[pos * block_rows + r, lo:hi], tiles.at[r, lo:hi, mine, :], loc_sem.at[stage]
            ).start()

    def send(stage):
        keep_own(stage)
        for cell in cells(stage):

            @pl.loop(1, cols_n)
            def _(k):
                send_cell(stage, cell, other(k))

    def edge_span(way, m):
        return (lower * block_rows + width + m, width - m, m + 1) if way == 0 else (
            upper * block_rows + m, 0, width - m)

    edge_to = (turned(upper), turned(lower))

    def send_edge(way):
        for m in range(width):
            r, lo, count = edge_span(way, m)
            src, dst = up.at[r, lo : lo + count], edge.at[m, :count, mine, :]

            @pl.when(col != edge_to[way])
            def _():
                pltpu.make_async_remote_copy(
                    src_ref=src,
                    dst_ref=dst,
                    send_sem=edge_send.at[way],
                    recv_sem=edge_recv.at[col],
                    device_id=(row, edge_to[way]),
                    device_id_type=MESH,
                ).start()

            @pl.when(col == edge_to[way])
            def _():
                pltpu.make_async_copy(src, dst, edge_recv.at[col]).start()

    def edge_piece(c):
        return tiles.at[: width // 2, : width + 1, slab_of(c), :]

    def arrive_edge():
        @pl.loop(0, cols_n)
        def _(c):
            piece = edge_piece(c)
            pltpu.make_async_copy(piece, piece, edge_recv.at[c]).wait()

    send(0)
    send_edge(0)
    send_edge(1)
    send(1)

    partner = cols_n - 1 - col
    occ_copy = pltpu.make_async_remote_copy(
        src_ref=occ,
        dst_ref=occ_far,
        send_sem=occ_sem.at[0],
        recv_sem=occ_sem.at[1],
        device_id=(row, partner),
        device_id_type=MESH,
    )
    occ_copy.start()
    occ_local = pltpu.make_async_copy(occ, occ_here, occ_sem.at[2])
    occ_local.start()
    occ_local.wait()
    occ_copy.wait()

    shape = kept.shape
    offset = (
        lax.broadcasted_iota(jnp.int32, shape, 0) + lax.broadcasted_iota(jnp.int32, shape, 1) + 1
    )
    total = rows_n * cols_n * block_rows
    chunk_far = row * cols_n + cols_n - 1 - pos
    flags_here, flags_far = occ_here[...], occ_far[...]
    for ref, flags, number in (
        (kept, jnp.where(odd == 1, flags_far, flags_here), chunk),
        (kept_far, jnp.where(odd == 1, flags_here, flags_far), chunk_far),
    ):
        ref[...] = jnp.where((flags == 1) & (number * block_rows + offset < total), 1, 0)

    def part_of(n):
        return slice(n * block, (n + 1) * block)

    @pl.when(jnp.logical_not(has_prev))
    def _():
        for q in range(width):
            strip[q, :, : (width - q) * block] = jnp.zeros(
                (block, (width - q) * block), strip.dtype
            )

    @pl.when(jnp.logical_not(has_next))
    def _():
        for m in range(width):
            strip[block_rows + m, :, width * block : (2 * width - m) * block] = jnp.zeros(
                (block, (width - m) * block), strip.dtype
            )

    def arrive(stage, then=None):
        piece = piece_of(stage, col)
        pltpu.make_async_copy(piece, piece, loc_sem.at[stage]).wait()

        @pl.loop(1, cols_n)
        def _(k):
            src = other(k)
            piece = piece_of(stage, src)
            pltpu.make_async_copy(piece, piece, in_recv.at[stage, src]).wait()
            if then is not None:
                for cell in cells(then):
                    send_cell(then, cell, src)

    def place(part):
        for d in range(width + 1):
            lo, hi = (
                (block_rows - d, block_rows),
                (0, width - d),
                (width - d, min(width + 1, block_rows - d)),
                (width + 1, block_rows - d),
            )[part]
            if lo >= hi:
                continue

            @pl.loop(lo, hi)
            def _(r):
                tile = tiles[r, d]
                if d == 0:
                    strip[r, :, part_of(width)] = symmetric(tile)
                else:
                    tile = masked(tile, kept[pl.ds(r, 1), :], d)
                    strip[r, :, part_of(width + d)] = tile
                    strip[r + d, :, part_of(width - d)] = tile.T

    def masked(tile, flags, d):
        return jnp.where(flags[:, d - 1 : d] == 1, tile, jnp.zeros_like(tile))

    def symmetric(tile):
        full = tile.astype(jnp.float32)
        return (0.5 * (full + full.T)).astype(strip.dtype)

    def place_upper():
        for m in range(width):
            for q in range(m + 1):
                flags = kept_far[width + m : width + m + 1, :]
                tile = masked(edge[m, q], flags, width - m + q)
                strip[q, :, part_of(m - q)] = tile.T

    def place_lower():
        for m in range(width):
            strip[block_rows + m, :, part_of(width)] = symmetric(edge[m, 0])
            for d in range(1, width - m):
                flags = kept_far[m : m + 1, :]
                strip[block_rows + m, :, part_of(width + d)] = masked(edge[m, d], flags, d)

    def halo(way, m):
        if way == 0:
            cut = slice(0, (width - m) * block)
            src, dst, dev = block_rows + m, m, next_dev
        else:
            cut = slice(width * block, (2 * width - m) * block)
            src, dst, dev = m, block_rows + m, prev_dev
        return pltpu.make_async_remote_copy(
            src_ref=strip.at[src, :, cut],
            dst_ref=strip.at[dst, :, cut],
            send_sem=halo_send.at[way, m],
            recv_sem=halo_recv.at[way, m],
            device_id=dev,
            device_id_type=MESH,
        )

    keep_own(2)
    arrive(0, then=2)
    place(0)

    @pl.when(pass_next)
    def _():
        for m in range(width):
            halo(0, m).start()

    place(1)

    @pl.when(pass_prev)
    def _():
        for m in range(width):
            halo(1, m).start()

    arrive(1)
    place(2)

    @pl.when(pass_prev)
    def _():
        for m in range(width):
            halo(0, m).wait_recv()

    @pl.when(pos == upper)
    def _():
        arrive_edge()
        place_upper()

    def products(r):
        flags = kept[pl.ds(r, 1), :]
        for e in range(width + 1):
            value = lax.dot_general(
                strip[r, :, e * block :],
                strip[r + e, :, : (2 * width + 1 - e) * block],
                (((1,), (1,)), ((), ())),
                preferred_element_type=jnp.float32,
            )
            if e > 0:
                value = jnp.where(flags[:, e - 1 : e] == 1, value, 0.0)
            prod[r, e] = value.astype(prod.dtype)
        place_row = pos * block_rows + r
        pltpu.make_async_copy(prod.at[r, :, mine, :], out.at[place_row], loc_sem.at[3]).start()

        @pl.loop(1, cols_n)
        def _(k):
            dst = other(k)
            pltpu.make_async_remote_copy(
                src_ref=prod.at[r, :, slab_of(dst), :],
                dst_ref=out.at[place_row],
                send_sem=out_send.at[dst],
                recv_sem=out_recv.at[col],
                device_id=(row, dst),
                device_id_type=MESH,
            ).start()

    products(0)
    arrive(2)
    place(3)

    @pl.when(pass_next)
    def _():
        for m in range(width):
            halo(1, m).wait_recv()

    @pl.when(pos == lower)
    def _():
        arrive_edge()
        place_lower()

    for d in range(1, width):

        @pl.loop(block_rows, block_rows + width - d)
        def _(r):
            strip[r + d, :, part_of(width - d)] = strip[r, :, part_of(width + d)].T

    pl.loop(1, block_rows)(products)

    @pl.when(pass_next)
    def _():
        for m in range(width):
            halo(0, m).wait_send()

    @pl.when(pass_prev)
    def _():
        for m in range(width):
            halo(1, m).wait_send()

    for way in range(2):

        @pl.when(col != edge_to[way])
        def _():
            piece = edge_piece(col)
            pltpu.make_async_copy(piece, piece, edge_send.at[way]).wait()

    def rows_of(c):
        return pl.ds(turned(c) * block_rows, block_rows)

    whole = out.at[rows_of(col)]
    pltpu.make_async_copy(whole, whole, loc_sem.at[3]).wait()

    @pl.loop(1, cols_n)
    def _(k):
        dev = other(k)
        sent = up.at[rows_of(dev)]
        pltpu.make_async_copy(sent, sent, in_send.at[dev]).wait()
        left = prod.at[:, :, slab_of(dev), :]
        pltpu.make_async_copy(left, left, out_send.at[dev]).wait()
        came = out.at[rows_of(dev)]
        pltpu.make_async_copy(came, came, out_recv.at[dev]).wait()


def shards(rows_n, cols_n, upper_tiles, occupied):
    block_rows, width = occupied.shape
    block = upper_tiles.shape[3]
    flags = jnp.pad(occupied, ((0, 0), (0, 128 - width)))
    dma = pltpu.SemaphoreType.DMA
    return pl.pallas_call(
        functools.partial(band_square_kernel, rows_n, cols_n, width),
        out_shape=jax.ShapeDtypeStruct(upper_tiles.shape, upper_tiles.dtype),
        in_specs=[pl.BlockSpec(memory_space=pl.ANY)] * 2,
        out_specs=pl.BlockSpec(memory_space=pl.ANY),
        scratch_shapes=[
            pltpu.VMEM((block_rows, width + 1, block, block), jnp.bfloat16),
            pltpu.VMEM((block_rows + width, block, (2 * width + 1) * block), jnp.bfloat16),
            pltpu.VMEM((block_rows, width + 1, block, block), jnp.bfloat16),
            pltpu.VMEM((width, width, block, block), jnp.bfloat16),
            pltpu.VMEM((block_rows, 128), jnp.int32),
            pltpu.VMEM((block_rows, 128), jnp.int32),
            pltpu.VMEM((block_rows, 128), jnp.int32),
            pltpu.VMEM((block_rows, 128), jnp.int32),
            dma((cols_n,)),
            dma((3, cols_n)),
            dma((2, width)),
            dma((2, width)),
            dma((2,)),
            dma((cols_n,)),
            dma((cols_n,)),
            dma((cols_n,)),
            dma((3,)),
            dma((4,)),
        ],
        compiler_params=pltpu.CompilerParams(
            collective_id=0, has_side_effects=True, vmem_limit_bytes=48 * 2**20
        ),
        cost_estimate=pl.CostEstimate(
            flops=2 * 35 * block_rows * block**3, bytes_accessed=2 * upper_tiles.size * 2, transcendentals=0
        ),
    )(upper_tiles, flags)


def solution(mesh):
    return jax.shard_map(
        functools.partial(shards, mesh.shape["row"], mesh.shape["col"]),
        mesh=mesh,
        in_specs=(P("row", None, "col", None), P(("row", "col"), None)),
        out_specs=P("row", None, "col", None),
        check_vma=False,
    )
```
